32 devices in a mesh: pts: 8 (over z, x), grp: 4 (over y, core).
Axes of the slice: x: 2, y: 2, z: 4, core: 2. Of those that a mesh axis runs over, the one named last changes fastest.
Arguments:
- vertex_features: bfloat16 [16384, 256], P(('pts', 'grp')), may hold values from -6 to 6
- result_cotangent: bfloat16 [16384, 256], P(('pts', 'grp')), may hold values from -6 to 6
- entry_matrix: bfloat16 [256, 256], replicated, may hold values from -0.375 to 0.375
- exit_matrix: bfloat16 [256, 256], replicated, may hold values from -0.375 to 0.375
- cluster_matrix: bfloat16 [32, 64], replicated, may hold values from -4 to 4
- softmax_sharpness: float32 [8], replicated, may hold values from 0.1 to 2
- cluster_attention_matrices: float32 [3, 32, 32], replicated, may hold values from -2 to 2
- occupied_tally: int32 [32], replicated, may hold values from 170 to 512, as said below
Outputs:
- x_grad: bfloat16 [16384, 256], P(('pts', 'grp'))
- weight_grads: float32 [2, 256, 256], P(None, 'grp')
- slice_grad: float32 [32, 64], replicated
- temp_grad: float32 [8], replicated
- token_grads: float32 [3, 32, 32], replicated
The draws below stay inside these ranges and needn't reach their ends.
Inputs may be any that keep to these rules, and one draw needn't show every extreme that they name: occupied_tally[i] is the number of valid points of the i-th block of 512 point slots; they come first in the block. Some block is full and some holds 170 in every draw.
All inputs are finite; a program needn't handle non-finite values.
Results may differ from the reference program's by a relative error of at most 0.012.
The reference program's roundings to bfloat16 on the way count: a program that leaves them out, or rounds other values in their place, can miss the bound.
Values may be sent and summed in bfloat16 or wider, within the bound.
No kernel may reach another device: no remote copies, remote signals or barrier semaphores. Data moves between devices by JAX's collectives and lax.ppermute only.
A program may use at most 64 MiB of HBM per device.

```python
import jax
import jax.numpy as jnp
from jax import lax

D = 256
H = 8
M = 64
PTS_DEV = 512
DH = 32
SHARDS = 32
POINTS = 16384


def draw_softmax_sharpness(key, part):
    base_key = jax.random.fold_in(key, 11)
    first_key, second_key, third_key = jax.random.split(base_key, 3)
    drawn_temp = jnp.exp(jax.random.uniform(first_key, (H,), jnp.float32, jnp.log(0.3), jnp.log(2.0)))
    order = jax.random.permutation(third_key, H)
    sharp = jnp.exp(jax.random.uniform(second_key, (H,), jnp.float32, jnp.log(0.15), jnp.log(0.3)))
    chosen = order < 1
    return jnp.where(chosen, sharp, drawn_temp).astype(jnp.float32)


def draw_cluster_matrix(key, part):
    base_key = jax.random.fold_in(key, 37)
    first_key, second_key = jax.random.split(base_key)
    column_scale = jnp.exp(jax.random.uniform(first_key, (1, M), jnp.float32, jnp.log(0.2), jnp.log(2.0)))
    entries = jax.random.truncated_normal(second_key, -4.0, 4.0, (DH, M), jnp.float32)
    return (entries * column_scale * (2.0 / DH) ** 0.5).astype(jnp.bfloat16)


def draw_occupied_tally(key, part):
    base_key = jax.random.fold_in(key, 23)
    first_key, second_key = jax.random.split(base_key)
    lowest = PTS_DEV // 3
    value_rows = jax.random.randint(first_key, (SHARDS,), lowest, PTS_DEV + 1, jnp.int32)
    order = jax.random.permutation(second_key, SHARDS)
    value_rows = jnp.where(order == 0, PTS_DEV, value_rows)
    value_rows = jnp.where(order == 1, lowest, value_rows)
    return value_rows.astype(jnp.int32)


def shard_levels(stream_key, dims, pieces, least, top_value):
    loudness, own = 1.0, jax.random.fold_in(stream_key, 6)
    for position, blocks in pieces:
        draws = jnp.exp(jax.random.uniform(jax.random.fold_in(own, position), (blocks,), jnp.float32, least / len(pieces), top_value / len(pieces)))
        loudness = loudness * jnp.repeat(draws, dims[position] // blocks).reshape([-1 if axis == position else 1 for axis in range(len(dims))])
    return loudness


def normal_values(rng, shape, deviation, reach, cuts=(), kind=jnp.bfloat16):
    result = jax.random.normal(rng, shape, jnp.float32) * deviation
    if len(cuts) > 0:
        result = shard_levels(rng, shape, cuts, -0.22, 0.18) * result
    return jnp.clip(result, min=-reach, max=reach).astype(kind)


def setup_inputs(seed: int = 0) -> dict:
    seeds = jax.random.split(jax.random.key(seed), 9)
    return {
        "vertex_features": normal_values(seeds[0], (POINTS, D), 1.0, 6.0, ((0, 32),)),
        "result_cotangent": normal_values(seeds[1], (POINTS, D), 1.0, 6.0, ((0, 32),)),
        "entry_matrix": normal_values(seeds[2], (D, D), D ** -0.5, 0.375),
        "exit_matrix": normal_values(seeds[3], (D, D), D ** -0.5, 0.375),
        "cluster_matrix": draw_cluster_matrix(jax.random.fold_in(seeds[8], 71), 0),
        "softmax_sharpness": draw_softmax_sharpness(jax.random.fold_in(seeds[8], 71), 0),
        "cluster_attention_matrices": normal_values(seeds[6], (3, DH, DH), (DH // 4) ** -0.5, 2.0, (), jnp.float32),
        "occupied_tally": draw_occupied_tally(jax.random.fold_in(seeds[8], 71), 0),
    }


def quantized_entries(value):
    return lax.optimization_barrier(value.astype(jnp.bfloat16)).astype(jnp.float32)


def segment_forward_sweep(feature_segment, result_cotangent_segment, validity_flags, entry_matrix, exit_matrix, cluster_matrix, softmax_sharpness):
    highest_precision = lax.Precision.HIGHEST
    point_rows = feature_segment.shape[0]
    attention_channels = softmax_sharpness.shape[0]
    single_features = quantized_entries(jnp.dot(feature_segment, entry_matrix, preferred_element_type=jnp.float32)).reshape(point_rows, attention_channels, -1)
    unscaled_product = jnp.einsum("phd,dm->phm", single_features, cluster_matrix.astype(jnp.float32), precision=highest_precision)
    cluster_scores = unscaled_product / softmax_sharpness[None, :, None]
    cluster_likelihood = jax.nn.softmax(cluster_scores, axis=-1)
    matrix_sequence = quantized_entries(cluster_likelihood * validity_flags[:, None, None])
    exit_cotangent = quantized_entries(jnp.dot(result_cotangent_segment, exit_matrix.T, preferred_element_type=jnp.float32)).reshape(point_rows, attention_channels, -1)
    return single_features, cluster_scores, cluster_likelihood, matrix_sequence, exit_cotangent


def segment_running_sums(feature_segment, result_cotangent_segment, validity_flags, entry_matrix, exit_matrix, cluster_matrix, softmax_sharpness):
    highest_precision = lax.Precision.HIGHEST
    single_features, cluster_scores, cluster_likelihood, matrix_sequence, exit_cotangent = segment_forward_sweep(feature_segment, result_cotangent_segment, validity_flags, entry_matrix, exit_matrix, cluster_matrix, softmax_sharpness)
    cluster_dividend = jnp.einsum("fzs,fzb->zsb", matrix_sequence, single_features, precision=highest_precision)
    cluster_normalizer = jnp.sum(matrix_sequence, axis=0)
    blended_cotangent = jnp.einsum("fzs,fzb->zsb", matrix_sequence, exit_cotangent, precision=highest_precision)
    return cluster_dividend, cluster_normalizer, blended_cotangent


def slice_middle(cluster_dividend, cluster_normalizer, blended_cotangent, cluster_attention_matrices):
    highest_precision = lax.Precision.HIGHEST
    clip = jnp.maximum(cluster_normalizer, 1.0)
    slice_tokens = cluster_dividend / clip[..., None]
    scale = slice_tokens.shape[-1] ** -0.5
    query_rows = jnp.einsum("cui,it->cut", slice_tokens, cluster_attention_matrices[0], precision=highest_precision)
    key_rows = jnp.einsum("cui,it->cut", slice_tokens, cluster_attention_matrices[1], precision=highest_precision)
    value_rows = jnp.einsum("cui,it->cut", slice_tokens, cluster_attention_matrices[2], precision=highest_precision)
    scores = jnp.einsum("hme,hne->hmn", query_rows, key_rows, precision=highest_precision) * scale
    attn = jax.nn.softmax(scores, axis=-1)
    mixed = jnp.einsum("hmn,hne->hme", attn, value_rows, precision=highest_precision)
    value_gradient = jnp.einsum("hmn,hme->hne", attn, blended_cotangent, precision=highest_precision)
    g_attn = jnp.einsum("hme,hne->hmn", blended_cotangent, value_rows, precision=highest_precision)
    g_scores = attn * (g_attn - jnp.sum(g_attn * attn, axis=-1, keepdims=True)) * scale
    query_gradient = jnp.einsum("hmn,hne->hme", g_scores, key_rows, precision=highest_precision)
    key_gradient = jnp.einsum("hmn,hme->hne", g_scores, query_rows, precision=highest_precision)
    query_map_gradient = jnp.einsum("sul,suv->lv", slice_tokens, query_gradient, precision=highest_precision)
    key_map_gradient = jnp.einsum("sul,suv->lv", slice_tokens, key_gradient, precision=highest_precision)
    value_map_gradient = jnp.einsum("sul,suv->lv", slice_tokens, value_gradient, precision=highest_precision)
    token_gradient = jnp.einsum("cqr,jr->cqj", query_gradient, cluster_attention_matrices[0], precision=highest_precision)
    token_gradient = token_gradient + jnp.einsum("cqr,jr->cqj", key_gradient, cluster_attention_matrices[1], precision=highest_precision)
    token_gradient = token_gradient + jnp.einsum("cqr,jr->cqj", value_gradient, cluster_attention_matrices[2], precision=highest_precision)
    g_num = token_gradient / clip[..., None]
    normalizer_cotangent = jnp.where(cluster_normalizer > 1.0, -jnp.sum(token_gradient * slice_tokens, axis=-1) / clip, 0.0)
    return mixed, g_num, normalizer_cotangent, jnp.stack([query_map_gradient, key_map_gradient, value_map_gradient])


def segment_backward_sweep(feature_segment, result_cotangent_segment, validity_flags, entry_matrix, exit_matrix, cluster_matrix, softmax_sharpness, blended_bottom_share, dividend_bottom_share, normalizer_cotangent):
    highest_precision = lax.Precision.HIGHEST
    point_rows = feature_segment.shape[0]
    single_features, cluster_scores, cluster_likelihood, matrix_sequence, exit_cotangent = segment_forward_sweep(feature_segment, result_cotangent_segment, validity_flags, entry_matrix, exit_matrix, cluster_matrix, softmax_sharpness)
    slice_weight = cluster_matrix.astype(jnp.float32)
    merged_heads = jnp.einsum("ibr,brw->ibw", matrix_sequence, blended_bottom_share, precision=highest_precision).reshape(point_rows, -1).astype(jnp.bfloat16)
    exit_matrix_cotangent = jnp.dot(merged_heads.T, result_cotangent_segment, preferred_element_type=jnp.float32)
    assign_weight_gradient = jnp.einsum("yos,ois->yoi", exit_cotangent, blended_bottom_share, precision=highest_precision)
    assign_weight_gradient = assign_weight_gradient + jnp.einsum("yos,ois->yoi", single_features, dividend_bottom_share, precision=highest_precision) + normalizer_cotangent[None]
    assign_weight_gradient = assign_weight_gradient * validity_flags[:, None, None]
    score_cotangent = cluster_likelihood * (assign_weight_gradient - jnp.sum(assign_weight_gradient * cluster_likelihood, axis=-1, keepdims=True))
    unscaled_cotangent = quantized_entries(score_cotangent / softmax_sharpness[None, :, None])
    float_input_gradient = jnp.einsum("ibr,brw->ibw", matrix_sequence, dividend_bottom_share, precision=highest_precision)
    float_input_gradient = float_input_gradient + jnp.einsum("phm,dm->phd", unscaled_cotangent, slice_weight, precision=highest_precision)
    cluster_matrix_cotangent = jnp.einsum("phd,phm->dm", single_features, unscaled_cotangent, precision=highest_precision)
    sharpness_cotangent = -jnp.sum(score_cotangent * cluster_scores, axis=(0, 2)) / softmax_sharpness
    g_xm = float_input_gradient.reshape(point_rows, -1).astype(jnp.bfloat16)
    feature_cotangent = jnp.dot(g_xm, entry_matrix.T, preferred_element_type=jnp.float32).astype(jnp.bfloat16)
    entry_matrix_cotangent = jnp.dot(feature_segment.T, g_xm, preferred_element_type=jnp.float32)
    return feature_cotangent, jnp.stack([entry_matrix_cotangent, exit_matrix_cotangent]), cluster_matrix_cotangent, sharpness_cotangent


def reference(vertex_features, result_cotangent, entry_matrix, exit_matrix, cluster_matrix, softmax_sharpness, cluster_attention_matrices, occupied_tally):
    shards = occupied_tally.shape[0]
    point_rows = vertex_features.shape[0] // shards
    width = vertex_features.shape[1]
    attention_channels = softmax_sharpness.shape[0]
    head = width // attention_channels
    slices = cluster_matrix.shape[1]
    blocks_x = vertex_features.reshape(shards, point_rows, width)
    blocks_dy = result_cotangent.reshape(shards, point_rows, width)
    live_all = (jnp.arange(point_rows, dtype=jnp.int32)[None, :] < occupied_tally[:, None]).astype(jnp.float32)

    def first(loop_state, item):
        feature_segment, result_cotangent_segment, validity_flags = item
        cluster_dividend, cluster_normalizer, blended_cotangent = segment_running_sums(feature_segment, result_cotangent_segment, validity_flags, entry_matrix, exit_matrix, cluster_matrix, softmax_sharpness)
        return (loop_state[0] + cluster_dividend, loop_state[1] + cluster_normalizer, loop_state[2] + blended_cotangent), None

    start = (jnp.zeros((attention_channels, slices, head), jnp.float32), jnp.zeros((attention_channels, slices), jnp.float32),
             jnp.zeros((attention_channels, slices, head), jnp.float32))
    totals, unused = lax.scan(first, start, (blocks_x, blocks_dy, live_all))
    mixed, g_num, normalizer_cotangent, token_grads = slice_middle(totals[0], totals[1], totals[2], cluster_attention_matrices)
    blended_bottom_share = quantized_entries(mixed)
    dividend_bottom_share = quantized_entries(g_num)

    def second(loop_state, item):
        feature_segment, result_cotangent_segment, validity_flags = item
        feature_cotangent, cotangent_sequence, cluster_matrix_cotangent, sharpness_cotangent = segment_backward_sweep(feature_segment, result_cotangent_segment, validity_flags, entry_matrix, exit_matrix, cluster_matrix, softmax_sharpness,
                                                           blended_bottom_share, dividend_bottom_share, normalizer_cotangent)
        return (loop_state[0] + cotangent_sequence, loop_state[1] + cluster_matrix_cotangent, loop_state[2] + sharpness_cotangent), feature_cotangent

    start2 = (jnp.zeros((2, width, width), jnp.float32), jnp.zeros((head, slices), jnp.float32),
              jnp.zeros((attention_channels,), jnp.float32))
    sums, x_grads = lax.scan(second, start2, (blocks_x, blocks_dy, live_all))
    x_grad = x_grads.reshape(shards * point_rows, width)
    return x_grad, sums[0], sums[1], sums[2], token_grads
```

```python
import jax
import jax.numpy as jnp
from jax import lax
from jax.experimental import pallas as pl
from jax.experimental.pallas import tpu as pltpu
from jax.sharding import PartitionSpec as P

F32 = jnp.float32
BF16 = jnp.bfloat16
ALL = ("pts", "grp")
LANES = 128
VMEM_LIMIT = 48 * 1024 * 1024
POINTS_LIMIT = 60 * 1024 * 1024


def dot(a, b):
    return lax.dot_general(a, b, (((1,), (0,)), ((), ())), preferred_element_type=F32)


def dot_nt(a, b):
    return lax.dot_general(a, b, (((1,), (1,)), ((), ())), preferred_element_type=F32)


def dot_tn(a, b):
    return lax.dot_general(a, b, (((0,), (0,)), ((), ())), preferred_element_type=F32)


def split(a):
    high = a.astype(BF16)
    return high, (a - high.astype(F32)).astype(BF16)


def dot3(product, a, b):
    return product(a[0], b[0]) + (product(a[1], b[0]) + product(a[0], b[1]))


def head_mask(shape, row_size, lane_size):
    rows = lax.broadcasted_iota(jnp.int32, shape, 0) // row_size
    lanes = lax.broadcasted_iota(jnp.int32, shape, 1) // lane_size
    return rows == lanes


def inverse_row(scalar_ref, index, length):
    return 1.0 / jnp.full((1, length), scalar_ref[index], F32)


def assign(sharp, x, entry, cluster, valid, xmt, weights, live_probs):
    points, width = x.shape
    heads = sharp.shape[0]
    head = width // heads
    slices = cluster.shape[1]
    xm = dot(x[...], entry[...]).astype(BF16)
    xmt[...] = xm.T
    cluster_t = cluster[...].T
    live = (lax.broadcasted_iota(jnp.int32, (1, points), 1) < valid).astype(F32)
    for h in range(heads):
        raw = dot(cluster_t, xmt[h * head : (h + 1) * head, :])
        logits = raw * inverse_row(sharp, h, points)
        e = jnp.exp(logits - jnp.max(logits, axis=0, keepdims=True))
        probs = e * (live / jnp.sum(e, axis=0, keepdims=True))
        if live_probs is not None:
            live_probs[h * slices : (h + 1) * slices, :] = probs
        weights[h * slices : (h + 1) * slices, :] = probs.astype(BF16)
    return xm


def valid_points(tally):
    return tally[lax.axis_index("pts") * lax.axis_size("grp") + lax.axis_index("grp")]


def points_kernel(
    tally_in,
    sharp_in,
    x_in,
    rc_in,
    entry_in,
    exit_in,
    cluster_in,
    payload,
    tally,
    sharp,
    x,
    rc,
    entry,
    exit_,
    cluster,
    xmt,
    weights,
    arrived,
):
    pairs = [
        (entry_in, entry),
        (x_in, x),
        (cluster_in, cluster),
        (sharp_in, sharp),
        (tally_in, tally),
        (exit_in, exit_),
        (rc_in, rc),
    ]
    copies = [
        pltpu.make_async_copy(source, target, arrived.at[i])
        for i, (source, target) in enumerate(pairs)
    ]
    for copy in copies:
        copy.start()
    points, width = x.shape
    heads = sharp.shape[0]
    head = width // heads
    slices = cluster.shape[1]
    per = LANES // head
    groups = heads // per
    for copy in copies:
        copy.wait()
    go = dot_nt(rc[...], exit_[...]).astype(BF16)
    xm = assign(sharp, x, entry, cluster, valid_points(tally), xmt, weights, None)
    rows = groups * slices
    lane_head = lax.broadcasted_iota(jnp.int32, (slices, 2 * LANES), 1) % LANES // head
    for g in range(groups):
        w = weights[g * per * slices : (g + 1) * per * slices, :]
        cut = slice(g * LANES, (g + 1) * LANES)
        full = dot(w, jnp.concatenate([xm[:, cut], go[:, cut]], axis=1))
        own = jnp.zeros((slices, 2 * LANES), F32)
        for j in range(per):
            own = jnp.where(lane_head == j, full[j * slices : (j + 1) * slices, :], own)
        payload[g * slices : (g + 1) * slices, :] = own[:, :LANES].astype(BF16)
        payload[rows + g * slices : rows + (g + 1) * slices, :] = own[:, LANES:].astype(BF16)
    ones = jnp.ones((heads, points), BF16)
    den = jnp.zeros((heads, rows), F32)
    head_row = lax.broadcasted_iota(jnp.int32, (heads, rows), 0)
    lane_group = lax.broadcasted_iota(jnp.int32, (heads, rows), 1) // slices
    for j in range(per):
        w = jnp.concatenate(
            [
                weights[(g * per + j) * slices : (g * per + j + 1) * slices, :]
                for g in range(groups)
            ],
            axis=0,
        )
        den = jnp.where(head_row == lane_group * per + j, dot_nt(ones, w), den)
    high = den.astype(BF16).astype(F32)
    payload[2 * rows :, :] = jnp.concatenate([high, den - high], axis=0).astype(BF16)


def shadow_kernel(
    tally,
    sharp,
    x,
    rc,
    entry,
    exit_,
    cluster,
    maps,
    payload_in,
    payload,
    xmt,
    got,
    weights,
    live_probs,
    maps_high,
    maps_low,
    cluster_rows,
):
    payload[...] = payload_in[...]
    assign(sharp, x, entry, cluster, valid_points(tally), xmt, weights, live_probs)
    got[...] = dot_nt(rc[...], exit_[...]).astype(BF16).T
    head = maps.shape[1]
    slices = cluster.shape[1]
    per = LANES // head
    mask = head_mask((LANES, LANES), head, head)
    for i in range(maps.shape[0]):
        a = jnp.concatenate([maps[i]] * per, axis=0)
        a = jnp.where(mask, jnp.concatenate([a] * per, axis=1), 0.0)
        high, low = split(a)
        maps_high[:, i * LANES : (i + 1) * LANES] = high
        maps_low[:, i * LANES : (i + 1) * LANES] = low
    c = cluster[...].astype(F32).T
    c = jnp.concatenate([c] * per, axis=1)
    c = jnp.concatenate([c] * per, axis=0)
    c = jnp.where(head_mask(c.shape, slices, head), c, 0.0)
    cluster_rows[...] = c.astype(BF16)


def middle_kernel(
    sharp,
    mine,
    other,
    maps_high,
    maps_low,
    cluster_rows,
    xmt,
    got,
    weights,
    live_probs,
    x,
    rc,
    keep,
    send,
    gxmt,
    tokens_out,
    grads_out,
    grad_rows,
):
    points, width = x.shape
    heads = sharp.shape[0]
    head = width // heads
    per = LANES // head
    groups = heads // per
    slices = cluster_rows.shape[0] // per
    rows = groups * slices
    scale = head**-0.5
    total = mine[...].astype(F32) + other[...].astype(F32)
    num = total[:rows]
    mixed_cotangent = total[rows : 2 * rows]
    den_rows = total[2 * rows : 2 * rows + heads] + total[2 * rows + heads : 2 * rows + 2 * heads]
    spread = (
        lax.broadcasted_iota(jnp.int32, (heads, LANES), 0) % per
        == lax.broadcasted_iota(jnp.int32, (heads, LANES), 1) // head
    ).astype(F32)
    d0 = den_rows.astype(BF16)
    rest = den_rows - d0.astype(F32)
    d1 = rest.astype(BF16)
    d2 = (rest - d1.astype(F32)).astype(BF16)
    spread = spread.astype(BF16)
    den = dot_tn(
        jnp.concatenate([d0.astype(F32), d1.astype(F32), d2.astype(F32)], axis=0).astype(BF16),
        jnp.concatenate([spread.astype(F32)] * 3, axis=0).astype(BF16),
    )
    clip_inverse = 1.0 / jnp.maximum(den, 1.0)
    tokens = num * clip_inverse
    tokens_out[...] = tokens
    maps = (maps_high[...], maps_low[...])
    qkv = dot3(dot, split(tokens), maps)
    wide = (LANES, per * slices)
    lane_mask = head_mask(wide, head, slices)
    row_mask = head_mask((per * slices, LANES), slices, head)

    def spread_heads(a):
        doubled = jnp.concatenate([a] * (LANES // slices), axis=0).T
        doubled = jnp.concatenate([doubled] * (per * slices // LANES), axis=1)
        return split(jnp.where(lane_mask, doubled, 0.0))

    def fold_heads(a):
        kept = jnp.where(row_mask, a, 0.0)
        out = kept[:slices]
        for j in range(1, per):
            out = out + kept[j * slices : (j + 1) * slices]
        return kept, out

    mixed_blocks, query_grads, key_grads, value_grads = [], [], [], []
    for g in range(groups):
        cut = slice(g * slices, (g + 1) * slices)
        q, k, v = (qkv[cut, i * LANES : (i + 1) * LANES] for i in range(3))
        gm = mixed_cotangent[cut]
        q_blocks, gm_blocks = spread_heads(q), spread_heads(gm)
        k2, v2 = split(k), split(v)
        scores = dot3(dot, k2, q_blocks) * scale
        g_attn = dot3(dot, v2, gm_blocks)
        e = jnp.exp(scores - jnp.max(scores, axis=0, keepdims=True))
        attn = e / jnp.sum(e, axis=0, keepdims=True)
        g_scores = attn * (g_attn - jnp.sum(g_attn * attn, axis=0, keepdims=True)) * scale
        attn2, gs2 = split(attn), split(g_scores)
        value_grads.append(dot3(dot_nt, attn2, gm_blocks))
        key_grads.append(dot3(dot_nt, gs2, q_blocks))
        attn_t, gs_t = split(attn.T), split(g_scores.T)
        query_grads.append(fold_heads(dot3(dot, gs_t, k2))[1])
        mixed_blocks.append(fold_heads(dot3(dot, attn_t, v2))[0].astype(BF16))
    grads = jnp.concatenate(
        [
            jnp.concatenate(query_grads, axis=0),
            jnp.concatenate(key_grads, axis=0),
            jnp.concatenate(value_grads, axis=0),
        ],
        axis=1,
    )
    grads_out[...] = grads
    token_cotangent = dot3(dot_nt, split(grads), maps)
    num_cotangent = token_cotangent * clip_inverse
    den_terms = jnp.where(den > 1.0, -token_cotangent * tokens * clip_inverse, 0.0)

    owners = grad_rows.shape[0]
    owner_rows = width // owners
    slice_sum = jnp.zeros((head, per * slices), F32)
    slice_mask = head_mask((LANES, per * slices), head, slices)
    temps = []
    for g in range(groups):
        cut = slice(g * slices, (g + 1) * slices)
        big = slice(g * per * slices, (g + 1) * per * slices)
        small = slice(g * LANES, (g + 1) * LANES)
        num_block = jnp.where(
            row_mask, jnp.concatenate([num_cotangent[cut]] * per, axis=0), 0.0
        ).astype(BF16)
        den_column = jnp.sum(
            jnp.where(row_mask, jnp.concatenate([den_terms[cut]] * per, axis=0), 0.0),
            axis=1,
            keepdims=True,
        )
        table = jnp.concatenate([mixed_blocks[g], num_block], axis=1)
        w = weights[big, :]
        xm_g = xmt[small, :]
        both = dot_tn(table, w)
        merged = both[:LANES].astype(BF16)
        grad_exit = dot(merged, rc[...])
        g_w = dot(table, jnp.concatenate([got[small, :], xm_g], axis=0)) + den_column
        raw = dot(cluster_rows[...], xm_g)
        g_raw = []
        for j in range(per):
            h = g * per + j
            part = slice(j * slices, (j + 1) * slices)
            lp = live_probs[h * slices : (h + 1) * slices, :]
            t = g_w[part] * lp
            g_logits = t - lp * jnp.sum(t, axis=0, keepdims=True)
            inverse = inverse_row(sharp, h, points)
            row = jnp.sum(g_logits * raw[part], axis=0, keepdims=True) * (inverse * inverse)
            temps.append(-row)
            g_raw.append((g_logits * inverse).astype(BF16))
        g_raw = jnp.concatenate(g_raw, axis=0)
        g_xm = (both[LANES:] + dot_tn(cluster_rows[...], g_raw)).astype(BF16)
        gxmt[small, :] = g_xm
        grad_entry = dot(g_xm, x[...]).T
        block = jnp.where(slice_mask, dot_nt(xm_g, g_raw), 0.0)
        for j in range(per):
            slice_sum = slice_sum + block[j * head : (j + 1) * head]
        for o in range(owners):
            grad_rows[o, :owner_rows, small] = grad_entry[
                o * owner_rows : (o + 1) * owner_rows
            ].astype(BF16)
        for r in range(g * LANES // owner_rows, (g + 1) * LANES // owner_rows):
            start = r * owner_rows - g * LANES
            grad_rows[r, owner_rows:, :] = grad_exit[start : start + owner_rows].astype(BF16)
    folded = slice_sum[:, :LANES]
    for i in range(1, per * slices // LANES):
        folded = folded + slice_sum[:, i * LANES : (i + 1) * LANES]
    half = head // 2
    temp = jnp.sum(jnp.concatenate(temps, axis=0), axis=1, keepdims=True)
    temp = jnp.broadcast_to(temp, (heads, width))
    temp_high = temp.astype(BF16).astype(F32)
    extra = jnp.concatenate(
        [jnp.concatenate([folded[:half], folded[half:]], axis=1), temp_high, temp - temp_high],
        axis=0,
    ).astype(BF16)
    odd = lax.axis_index("grp") % 2
    chunk = 2 * owner_rows
    for i in range(owners // 2):
        keep[i * chunk : (i + 1) * chunk, :] = grad_rows[2 * i + odd]
        send[i * chunk : (i + 1) * chunk, :] = grad_rows[2 * i + 1 - odd]
    keep[owners // 2 * chunk :, :] = extra
    send[owners // 2 * chunk :, :] = extra


def features_kernel(gxmt, entry, tokens, grads, x_grad, token_grads):
    x_grad[...] = dot_nt(gxmt[...].T, entry[...]).astype(BF16)
    maps, head = token_grads.shape[:2]
    per = LANES // head
    full = dot3(dot, split(tokens[...].T), split(grads[...]))
    for i in range(maps):
        part = full[:, i * LANES : (i + 1) * LANES]
        part = jnp.where(head_mask((LANES, LANES), head, head), part, 0.0)
        out = part[:head]
        for j in range(1, per):
            out = out + part[j * head : (j + 1) * head]
        shift = LANES // 2
        while shift >= head:
            out = out + pltpu.roll(out, shift, 1)
            shift //= 2
        token_grads[i] = out[:, :head]


def finish_kernel(mine, other, weight_grads, slice_grad, temp_grad):
    total = mine[...].astype(F32) + other[...].astype(F32)
    owner_rows = weight_grads.shape[1]
    head, slices = slice_grad.shape
    weight_grads[0] = total[:owner_rows]
    weight_grads[1] = total[owner_rows : 2 * owner_rows]
    half = head // 2
    extra = total[2 * owner_rows :]
    folded = jnp.concatenate([extra[:half, :LANES], extra[:half, LANES : 2 * LANES]], axis=0)
    shift = LANES // 2
    while shift >= slices:
        folded = folded + pltpu.roll(folded, shift, 1)
        shift //= 2
    slice_grad[...] = folded[:, :slices]
    heads = temp_grad.shape[1]
    temp = (extra[half : half + heads] + extra[half + heads : half + 2 * heads])[:, :LANES]
    temp = jnp.where(head_mask(temp.shape, 1, 1), temp, 0.0)
    temp_grad[...] = jnp.sum(temp, axis=0, keepdims=True)[:, :heads]


def call(kernel, shapes, in_smem, count, scratch=(), space=pltpu.VMEM, limit=VMEM_LIMIT):
    smem = pl.BlockSpec(memory_space=pltpu.SMEM)
    vmem = pl.BlockSpec(memory_space=pltpu.VMEM)
    rest = pl.BlockSpec(memory_space=space)
    return pl.pallas_call(
        kernel,
        out_shape=[jax.ShapeDtypeStruct(s, d) for s, d in shapes],
        in_specs=[smem] * in_smem + [rest] * (count - in_smem),
        out_specs=[vmem] * len(shapes),
        scratch_shapes=list(scratch),
        compiler_params=pltpu.CompilerParams(vmem_limit_bytes=limit),
    )


def exchange(a, mask):
    devices = lax.axis_size("pts") * lax.axis_size("grp")
    return lax.ppermute(a, ALL, [(i, i ^ mask) for i in range(devices)])


def halves(total, start):
    pair = total[start:]
    n = pair.shape[0] // 2
    pair = pair[:n] + pair[n:]
    high = lax.reduce_precision(pair, 8, 7)
    return jnp.concatenate([total[:start], high, pair - high], axis=0).astype(BF16)


def local(x, rc, entry, exit_, cluster, sharp, maps, tally):
    points, width = x.shape
    heads = sharp.shape[0]
    head, slices = cluster.shape
    owners = lax.axis_size("grp")
    devices = lax.axis_size("pts") * owners
    per = LANES // head
    rows = heads // per * slices
    token_rows = 2 * rows + 2 * heads
    (payload,) = call(
        points_kernel,
        [((token_rows, LANES), BF16)],
        0,
        7,
        scratch=[
            pltpu.SMEM(tally.shape, tally.dtype),
            pltpu.SMEM(sharp.shape, sharp.dtype),
            *(pltpu.VMEM(a.shape, a.dtype) for a in (x, rc, entry, exit_, cluster)),
            pltpu.VMEM((width, points), BF16),
            pltpu.VMEM((heads * slices, points), BF16),
            pltpu.SemaphoreType.DMA((7,)),
        ],
        space=pltpu.HBM,
        limit=POINTS_LIMIT,
    )(tally, sharp, x, rc, entry, exit_, cluster)
    other = exchange(payload, 8)
    mine, xmt, got, weights, live_probs, maps_high, maps_low, cluster_rows = call(
        shadow_kernel,
        [
            ((token_rows, LANES), BF16),
            ((width, points), BF16),
            ((width, points), BF16),
            ((heads * slices, points), BF16),
            ((heads * slices, points), F32),
            ((LANES, 3 * LANES), BF16),
            ((LANES, 3 * LANES), BF16),
            ((per * slices, LANES), BF16),
        ],
        2,
        9,
    )(tally, sharp, x, rc, entry, exit_, cluster, maps, payload)
    mine = halves(mine.astype(F32) + other.astype(F32), 2 * rows)
    mask = 16
    while mask < devices:
        other = exchange(mine, mask)
        mine = halves(mine.astype(F32) + other.astype(F32), 2 * rows)
        mask *= 2
    far, b, a = exchange(mine, 6), exchange(mine, 2), exchange(mine, 4)
    mine = halves(
        (mine.astype(F32) + a.astype(F32)) + (b.astype(F32) + far.astype(F32)), 2 * rows
    )
    other = exchange(mine, 1)

    owner_rows = width // owners
    chunk = 2 * owner_rows
    extra = head // 2 + 2 * heads
    keep, send, gxmt, tokens, grads = call(
        middle_kernel,
        [
            ((owners // 2 * chunk + extra, width), BF16),
            ((owners // 2 * chunk + extra, width), BF16),
            ((width, points), BF16),
            ((rows, LANES), F32),
            ((rows, 3 * LANES), F32),
        ],
        1,
        12,
        scratch=[pltpu.VMEM((owners, chunk, width), BF16)],
    )(
        sharp,
        mine,
        other,
        maps_high,
        maps_low,
        cluster_rows,
        xmt,
        got,
        weights,
        live_probs,
        x,
        rc,
    )

    got_half = exchange(send, 1)
    x_grad, token_grads = call(
        features_kernel,
        [((points, width), BF16), (maps.shape, F32)],
        0,
        4,
    )(gxmt, entry, tokens, grads)
    total = keep.astype(F32) + got_half.astype(F32)
    total = halves(total, total.shape[0] - 2 * heads)
    half = lax.axis_index("grp") // 2
    common = total[owners // 2 * chunk :]
    mine = jnp.concatenate(
        [lax.dynamic_slice_in_dim(total, half * chunk, chunk), common], axis=0
    )
    theirs = jnp.concatenate(
        [lax.dynamic_slice_in_dim(total, (1 - half) * chunk, chunk), common], axis=0
    )
    far, b, a = exchange(theirs, 6), exchange(theirs, 2), exchange(mine, 4)
    total = (mine.astype(F32) + a.astype(F32)) + (b.astype(F32) + far.astype(F32))
    mine = halves(total, total.shape[0] - 2 * heads)
    mask = 8
    while 2 * mask < devices:
        other = exchange(mine, mask)
        total = mine.astype(F32) + other.astype(F32)
        mine = halves(total, total.shape[0] - 2 * heads)
        mask *= 2
    other = exchange(mine, mask)
    weight_grads, slice_grad, temp_grad = call(
        finish_kernel,
        [
            ((2, owner_rows, width), F32),
            ((head, slices), F32),
            ((1, heads), F32),
        ],
        0,
        2,
    )(mine, other)
    return x_grad, weight_grads, slice_grad, temp_grad.reshape(heads), token_grads


def solution(mesh):
    return jax.shard_map(
        local,
        mesh=mesh,
        in_specs=(P(ALL, None), P(ALL, None), P(), P(), P(), P(), P(), P()),
        out_specs=(P(ALL, None), P(None, "grp", None), P(), P(), P()),
        check_vma=False,
    )
```

```python
import math

import jax
import jax.numpy as jnp
from jax import lax
from jax.experimental import pallas as pl
from jax.experimental.pallas import tpu as pltpu
from jax.sharding import PartitionSpec as P

F32 = jnp.float32
BF16 = jnp.bfloat16
ALL = ("pts", "grp")
LANES = 128
VMEM_LIMIT = 48 * 1024 * 1024
POINTS_LIMIT = 60 * 1024 * 1024


def dot(a, b):
    return lax.dot_general(a, b, (((1,), (0,)), ((), ())), preferred_element_type=F32)


def dot_nt(a, b):
    return lax.dot_general(a, b, (((1,), (1,)), ((), ())), preferred_element_type=F32)


def dot_tn(a, b):
    return lax.dot_general(a, b, (((0,), (0,)), ((), ())), preferred_element_type=F32)


def split(a):
    high = a.astype(BF16)
    return high, (a - high.astype(F32)).astype(BF16)


def dot3(product, a, b):
    return product(a[0], b[0]) + (product(a[1], b[0]) + product(a[0], b[1]))


def head_mask(shape, row_size, lane_size):
    rows = lax.broadcasted_iota(jnp.int32, shape, 0) // row_size
    lanes = lax.broadcasted_iota(jnp.int32, shape, 1) // lane_size
    return rows == lanes


def inverse_row(scalar_ref, index, length):
    return 1.0 / jnp.full((1, length), scalar_ref[index], F32)


def assign(sharp, x, entry, cluster, valid, xmt, weights, live_probs):
    points, width = x.shape
    heads = sharp.shape[0]
    head = width // heads
    slices = cluster.shape[1]
    xm = dot(x[...], entry[...]).astype(BF16)
    xmt[...] = xm.T
    cluster_t = cluster[...].T
    live = (lax.broadcasted_iota(jnp.int32, (1, points), 1) < valid).astype(F32)
    for h in range(heads):
        raw = dot(cluster_t, xmt[h * head : (h + 1) * head, :])
        logits = raw * inverse_row(sharp, h, points)
        e = jnp.exp(logits - jnp.max(logits, axis=0, keepdims=True))
        probs = e * (live / jnp.sum(e, axis=0, keepdims=True))
        if live_probs is not None:
            live_probs[h * slices : (h + 1) * slices, :] = probs
        weights[h * slices : (h + 1) * slices, :] = probs.astype(BF16)
    return xm


def valid_points(tally):
    return tally[lax.axis_index("pts") * lax.axis_size("grp") + lax.axis_index("grp")]


def points_kernel(
    tally_in,
    sharp_in,
    x_in,
    rc_in,
    entry_in,
    exit_in,
    cluster_in,
    payload,
    tally,
    sharp,
    x,
    rc,
    entry,
    exit_,
    cluster,
    xmt,
    weights,
    arrived,
):
    pairs = [
        (entry_in, entry),
        (x_in, x),
        (cluster_in, cluster),
        (sharp_in, sharp),
        (tally_in, tally),
        (exit_in, exit_),
        (rc_in, rc),
    ]
    copies = [
        pltpu.make_async_copy(source, target, arrived.at[i])
        for i, (source, target) in enumerate(pairs)
    ]
    for copy in copies:
        copy.start()
    points, width = x.shape
    heads = sharp.shape[0]
    head = width // heads
    slices = cluster.shape[1]
    per = LANES // head
    groups = heads // per
    for copy in copies:
        copy.wait()
    go = dot_nt(rc[...], exit_[...]).astype(BF16)
    xm = assign(sharp, x, entry, cluster, valid_points(tally), xmt, weights, None)
    rows = groups * slices
    lane_head = lax.broadcasted_iota(jnp.int32, (slices, 2 * LANES), 1) % LANES // head
    for g in range(groups):
        w = weights[g * per * slices : (g + 1) * per * slices, :]
        cut = slice(g * LANES, (g + 1) * LANES)
        full = dot(w, jnp.concatenate([xm[:, cut], go[:, cut]], axis=1))
        own = jnp.zeros((slices, 2 * LANES), F32)
        for j in range(per):
            own = jnp.where(lane_head == j, full[j * slices : (j + 1) * slices, :], own)
        payload[g * slices : (g + 1) * slices, :] = own[:, :LANES].astype(BF16)
        payload[rows + g * slices : rows + (g + 1) * slices, :] = own[:, LANES:].astype(BF16)
    ones = jnp.ones((heads, points), BF16)
    den = jnp.zeros((heads, rows), F32)
    head_row = lax.broadcasted_iota(jnp.int32, (heads, rows), 0)
    lane_group = lax.broadcasted_iota(jnp.int32, (heads, rows), 1) // slices
    for j in range(per):
        w = jnp.concatenate(
            [
                weights[(g * per + j) * slices : (g * per + j + 1) * slices, :]
                for g in range(groups)
            ],
            axis=0,
        )
        den = jnp.where(head_row == lane_group * per + j, dot_nt(ones, w), den)
    high = den.astype(BF16).astype(F32)
    payload[2 * rows :, :] = jnp.concatenate([high, den - high], axis=0).astype(BF16)


def shadow_kernel(
    tally,
    sharp,
    x,
    rc,
    entry,
    exit_,
    cluster,
    maps,
    payload_in,
    payload,
    xmt,
    got,
    weights,
    live_probs,
    maps_high,
    maps_low,
    cluster_rows,
):
    payload[...] = payload_in[...]
    assign(sharp, x, entry, cluster, valid_points(tally), xmt, weights, live_probs)
    got[...] = dot_nt(rc[...], exit_[...]).astype(BF16).T
    head = maps.shape[1]
    slices = cluster.shape[1]
    per = LANES // head
    mask = head_mask((LANES, LANES), head, head)
    for i in range(maps.shape[0]):
        a = jnp.concatenate([maps[i]] * per, axis=0)
        a = jnp.where(mask, jnp.concatenate([a] * per, axis=1), 0.0)
        high, low = split(a)
        maps_high[:, i * LANES : (i + 1) * LANES] = high
        maps_low[:, i * LANES : (i + 1) * LANES] = low
    c = cluster[...].astype(F32).T
    c = jnp.concatenate([c] * per, axis=1)
    c = jnp.concatenate([c] * per, axis=0)
    c = jnp.where(head_mask(c.shape, slices, head), c, 0.0)
    cluster_rows[...] = c.astype(BF16)


def middle_kernel(
    sharp,
    mine,
    other,
    maps_high,
    maps_low,
    cluster_rows,
    xmt,
    got,
    weights,
    live_probs,
    x,
    rc,
    keep,
    send,
    gxmt,
    tokens_out,
    grads_out,
    grad_rows,
):
    points, width = x.shape
    heads = sharp.shape[0]
    head = width // heads
    per = LANES // head
    groups = heads // per
    slices = cluster_rows.shape[0] // per
    rows = groups * slices
    scale = head**-0.5
    total = mine[...].astype(F32) + other[...].astype(F32)
    num = total[:rows]
    mixed_cotangent = total[rows : 2 * rows]
    den_rows = total[2 * rows : 2 * rows + heads] + total[2 * rows + heads : 2 * rows + 2 * heads]
    spread = (
        lax.broadcasted_iota(jnp.int32, (heads, LANES), 0) % per
        == lax.broadcasted_iota(jnp.int32, (heads, LANES), 1) // head
    ).astype(F32)
    d0 = den_rows.astype(BF16)
    rest = den_rows - d0.astype(F32)
    d1 = rest.astype(BF16)
    d2 = (rest - d1.astype(F32)).astype(BF16)
    spread = spread.astype(BF16)
    den = dot_tn(
        jnp.concatenate([d0.astype(F32), d1.astype(F32), d2.astype(F32)], axis=0).astype(BF16),
        jnp.concatenate([spread.astype(F32)] * 3, axis=0).astype(BF16),
    )
    clip_inverse = 1.0 / jnp.maximum(den, 1.0)
    tokens = num * clip_inverse
    tokens_out[...] = tokens
    maps = (maps_high[...], maps_low[...])
    qkv = dot3(dot, split(tokens), maps)
    wide = (LANES, per * slices)
    lane_mask = head_mask(wide, head, slices)
    row_mask = head_mask((per * slices, LANES), slices, head)

    def spread_heads(a):
        doubled = jnp.concatenate([a] * (LANES // slices), axis=0).T
        doubled = jnp.concatenate([doubled] * (per * slices // LANES), axis=1)
        return split(jnp.where(lane_mask, doubled, 0.0))

    def fold_heads(a):
        kept = jnp.where(row_mask, a, 0.0)
        out = kept[:slices]
        for j in range(1, per):
            out = out + kept[j * slices : (j + 1) * slices]
        return kept, out

    mixed_blocks, query_grads, key_grads, value_grads = [], [], [], []
    for g in range(groups):
        cut = slice(g * slices, (g + 1) * slices)
        q, k, v = (qkv[cut, i * LANES : (i + 1) * LANES] for i in range(3))
        gm = mixed_cotangent[cut]
        q_blocks, gm_blocks = spread_heads(q), spread_heads(gm)
        k2, v2 = split(k), split(v)
        scores = dot3(dot, k2, q_blocks) * scale
        g_attn = dot3(dot, v2, gm_blocks)
        e = jnp.exp(scores - jnp.max(scores, axis=0, keepdims=True))
        attn = e / jnp.sum(e, axis=0, keepdims=True)
        g_scores = attn * (g_attn - jnp.sum(g_attn * attn, axis=0, keepdims=True)) * scale
        attn2, gs2 = split(attn), split(g_scores)
        value_grads.append(dot3(dot_nt, attn2, gm_blocks))
        key_grads.append(dot3(dot_nt, gs2, q_blocks))
        attn_t, gs_t = split(attn.T), split(g_scores.T)
        query_grads.append(fold_heads(dot3(dot, gs_t, k2))[1])
        mixed_blocks.append(fold_heads(dot3(dot, attn_t, v2))[0].astype(BF16))
    grads = jnp.concatenate(
        [
            jnp.concatenate(query_grads, axis=0),
            jnp.concatenate(key_grads, axis=0),
            jnp.concatenate(value_grads, axis=0),
        ],
        axis=1,
    )
    grads_out[...] = grads
    token_cotangent = dot3(dot_nt, split(grads), maps)
    num_cotangent = token_cotangent * clip_inverse
    den_terms = jnp.where(den > 1.0, -token_cotangent * tokens * clip_inverse, 0.0)

    owners = grad_rows.shape[0]
    owner_rows = width // owners
    slice_sum = jnp.zeros((head, per * slices), F32)
    slice_mask = head_mask((LANES, per * slices), head, slices)
    temps = []
    for g in range(groups):
        cut = slice(g * slices, (g + 1) * slices)
        big = slice(g * per * slices, (g + 1) * per * slices)
        small = slice(g * LANES, (g + 1) * LANES)
        num_block = jnp.where(
            row_mask, jnp.concatenate([num_cotangent[cut]] * per, axis=0), 0.0
        ).astype(BF16)
        den_column = jnp.sum(
            jnp.where(row_mask, jnp.concatenate([den_terms[cut]] * per, axis=0), 0.0),
            axis=1,
            keepdims=True,
        )
        table = jnp.concatenate([mixed_blocks[g], num_block], axis=1)
        w = weights[big, :]
        xm_g = xmt[small, :]
        both = dot_tn(table, w)
        merged = both[:LANES].astype(BF16)
        grad_exit = dot(merged, rc[...])
        g_w = dot(table, jnp.concatenate([got[small, :], xm_g], axis=0)) + den_column
        raw = dot(cluster_rows[...], xm_g)
        g_raw = []
        for j in range(per):
            h = g * per + j
            part = slice(j * slices, (j + 1) * slices)
            lp = live_probs[h * slices : (h + 1) * slices, :]
            t = g_w[part] * lp
            g_logits = t - lp * jnp.sum(t, axis=0, keepdims=True)
            inverse = inverse_row(sharp, h, points)
            row = jnp.sum(g_logits * raw[part], axis=0, keepdims=True) * (inverse * inverse)
            temps.append(-row)
            g_raw.append((g_logits * inverse).astype(BF16))
        g_raw = jnp.concatenate(g_raw, axis=0)
        g_xm = (both[LANES:] + dot_tn(cluster_rows[...], g_raw)).astype(BF16)
        gxmt[small, :] = g_xm
        grad_entry = dot(g_xm, x[...]).T
        block = jnp.where(slice_mask, dot_nt(xm_g, g_raw), 0.0)
        for j in range(per):
            slice_sum = slice_sum + block[j * head : (j + 1) * head]
        for o in range(owners):
            grad_rows[o, :owner_rows, small] = grad_entry[
                o * owner_rows : (o + 1) * owner_rows
            ].astype(BF16)
        for r in range(g * LANES // owner_rows, (g + 1) * LANES // owner_rows):
            start = r * owner_rows - g * LANES
            grad_rows[r, owner_rows:, :] = grad_exit[start : start + owner_rows].astype(BF16)
    folded = slice_sum[:, :LANES]
    for i in range(1, per * slices // LANES):
        folded = folded + slice_sum[:, i * LANES : (i + 1) * LANES]
    half = head // 2
    temp = jnp.sum(jnp.concatenate(temps, axis=0), axis=1, keepdims=True)
    temp = jnp.broadcast_to(temp, (heads, width))
    temp_high = temp.astype(BF16).astype(F32)
    extra = jnp.concatenate(
        [jnp.concatenate([folded[:half], folded[half:]], axis=1), temp_high, temp - temp_high],
        axis=0,
    ).astype(BF16)
    odd = lax.axis_index("grp") % 2
    chunk = 2 * owner_rows
    for i in range(owners // 2):
        keep[i * chunk : (i + 1) * chunk, :] = grad_rows[2 * i + odd]
        send[i * chunk : (i + 1) * chunk, :] = grad_rows[2 * i + 1 - odd]
    keep[owners // 2 * chunk :, :] = extra
    send[owners // 2 * chunk :, :] = extra


def features_kernel(gxmt, entry, tokens, grads, x_grad, token_grads):
    x_grad[...] = dot_nt(gxmt[...].T, entry[...]).astype(BF16)
    maps, head = token_grads.shape[:2]
    per = LANES // head
    full = dot3(dot, split(tokens[...].T), split(grads[...]))
    for i in range(maps):
        part = full[:, i * LANES : (i + 1) * LANES]
        part = jnp.where(head_mask((LANES, LANES), head, head), part, 0.0)
        out = part[:head]
        for j in range(1, per):
            out = out + part[j * head : (j + 1) * head]
        shift = LANES // 2
        while shift >= head:
            out = out + pltpu.roll(out, shift, 1)
            shift //= 2
        token_grads[i] = out[:, :head]


def finish_kernel(mine, other, weight_grads, slice_grad, temp_grad):
    total = mine[...].astype(F32) + other[...].astype(F32)
    owner_rows = weight_grads.shape[1]
    head, slices = slice_grad.shape
    weight_grads[0] = total[:owner_rows]
    weight_grads[1] = total[owner_rows : 2 * owner_rows]
    half = head // 2
    extra = total[2 * owner_rows :]
    folded = jnp.concatenate([extra[:half, :LANES], extra[:half, LANES : 2 * LANES]], axis=0)
    shift = LANES // 2
    while shift >= slices:
        folded = folded + pltpu.roll(folded, shift, 1)
        shift //= 2
    slice_grad[...] = folded[:, :slices]
    heads = temp_grad.shape[1]
    temp = (extra[half : half + heads] + extra[half + heads : half + 2 * heads])[:, :LANES]
    temp = jnp.where(head_mask(temp.shape, 1, 1), temp, 0.0)
    temp_grad[...] = jnp.sum(temp, axis=0, keepdims=True)[:, :heads]


def call(kernel, shapes, in_smem, count, scratch=(), space=pltpu.VMEM, limit=VMEM_LIMIT):
    smem = pl.BlockSpec(memory_space=pltpu.SMEM)
    vmem = pl.BlockSpec(memory_space=pltpu.VMEM)
    rest = pl.BlockSpec(memory_space=space)
    return pl.pallas_call(
        kernel,
        out_shape=[jax.ShapeDtypeStruct(s, d) for s, d in shapes],
        in_specs=[smem] * in_smem + [rest] * (count - in_smem),
        out_specs=[vmem] * len(shapes),
        scratch_shapes=list(scratch),
        compiler_params=pltpu.CompilerParams(vmem_limit_bytes=limit),
    )


def exchange(a, mask):
    devices = lax.axis_size("pts") * lax.axis_size("grp")
    return lax.ppermute(a, ALL, [(i, i ^ mask) for i in range(devices)])


def exchanges(a, masks):
    return [exchange(a, mask) for mask in masks]


def gather(mine, others):
    mine, others = mine.astype(F32), [a.astype(F32) for a in others]
    if len(others) == 1:
        return mine + others[0]
    return (mine + others[0]) + (others[1] + others[2])


def token_pack(values, start, root_scale, den_scale):
    sums, pair = values[:start], values[start:]
    n = pair.shape[0] // 2
    pair = (pair[:n] + pair[n:]) * den_scale
    high = lax.reduce_precision(pair, 8, 7)
    roots = jnp.sqrt(jnp.abs(sums)) * root_scale
    roots = jnp.where(sums < 0.0, -roots, roots)
    return jnp.concatenate([roots, high, pair - high], axis=0).astype(jnp.float16)


def token_unpack(packed, start, root_scale, den_scale):
    packed = packed.astype(F32)
    row = lax.broadcasted_iota(jnp.int32, packed.shape, 0)
    return packed * jnp.where(row < start, jnp.abs(packed) * root_scale**-2, 1.0 / den_scale)


def halves(total, start):
    pair = total[start:]
    n = pair.shape[0] // 2
    pair = pair[:n] + pair[n:]
    high = lax.reduce_precision(pair, 8, 7)
    return jnp.concatenate([total[:start], high, pair - high], axis=0).astype(BF16)


def local(x, rc, entry, exit_, cluster, sharp, maps, tally):
    points, width = x.shape
    heads = sharp.shape[0]
    head, slices = cluster.shape
    owners = lax.axis_size("grp")
    devices = lax.axis_size("pts") * owners
    per = LANES // head
    rows = heads // per * slices
    token_rows = 2 * rows + 2 * heads
    far = [1 << bit for bit in range(4, devices.bit_length() - 1)]
    (payload,) = call(
        points_kernel,
        [((token_rows, LANES), BF16)],
        0,
        7,
        scratch=[
            pltpu.SMEM(tally.shape, tally.dtype),
            pltpu.SMEM(sharp.shape, sharp.dtype),
            *(pltpu.VMEM(a.shape, a.dtype) for a in (x, rc, entry, exit_, cluster)),
            pltpu.VMEM((width, points), BF16),
            pltpu.VMEM((heads * slices, points), BF16),
            pltpu.SemaphoreType.DMA((7,)),
        ],
        space=pltpu.HBM,
        limit=POINTS_LIMIT,
    )(tally, sharp, x, rc, entry, exit_, cluster)
    steps = ((8,), *((mask,) for mask in far), (2, 4, 6), (1,))
    all_points = devices * points
    root_scale = 2.0 ** math.floor(math.log2(65000.0 / math.sqrt(all_points * width * 2.25)))
    den_scale = 2.0 ** -max(0, math.ceil(math.log2(all_points / 2.0**15)))
    others = exchanges(payload, steps[0])
    mine, xmt, got, weights, live_probs, maps_high, maps_low, cluster_rows = call(
        shadow_kernel,
        [
            ((token_rows, LANES), BF16),
            ((width, points), BF16),
            ((width, points), BF16),
            ((heads * slices, points), BF16),
            ((heads * slices, points), F32),
            ((LANES, 3 * LANES), BF16),
            ((LANES, 3 * LANES), BF16),
            ((per * slices, LANES), BF16),
        ],
        2,
        9,
    )(tally, sharp, x, rc, entry, exit_, cluster, maps, payload)
    total = gather(mine, others)
    for masks in steps[1:-1]:
        mine = token_pack(total, 2 * rows, root_scale, den_scale)
        others = exchanges(mine, masks)
        mine, *others = (
            token_unpack(a, 2 * rows, root_scale, den_scale) for a in (mine, *others)
        )
        total = gather(mine, others)
    mine = total
    (other,) = exchanges(mine, steps[-1])

    owner_rows = width // owners
    chunk = 2 * owner_rows
    extra = head // 2 + 2 * heads
    keep, send, gxmt, tokens, grads = call(
        middle_kernel,
        [
            ((owners // 2 * chunk + extra, width), BF16),
            ((owners // 2 * chunk + extra, width), BF16),
            ((width, points), BF16),
            ((rows, LANES), F32),
            ((rows, 3 * LANES), F32),
        ],
        1,
        12,
        scratch=[pltpu.VMEM((owners, chunk, width), BF16)],
    )(
        sharp,
        mine,
        other,
        maps_high,
        maps_low,
        cluster_rows,
        xmt,
        got,
        weights,
        live_probs,
        x,
        rc,
    )

    got_half = exchange(send, 1)
    x_grad, token_grads = call(
        features_kernel,
        [((points, width), BF16), (maps.shape, F32)],
        0,
        4,
    )(gxmt, entry, tokens, grads)
    total = keep.astype(F32) + got_half.astype(F32)
    total = halves(total, total.shape[0] - 2 * heads)
    half = lax.axis_index("grp") // 2
    common = total[owners // 2 * chunk :]
    mine = jnp.concatenate(
        [lax.dynamic_slice_in_dim(total, half * chunk, chunk), common], axis=0
    )
    theirs = jnp.concatenate(
        [lax.dynamic_slice_in_dim(total, (1 - half) * chunk, chunk), common], axis=0
    )
    others = [exchange(mine, 4), exchange(theirs, 2), exchange(theirs, 6)]
    total = gather(mine, others)
    mine = halves(total, total.shape[0] - 2 * heads)
    for mask in (8, *far[:-1]):
        total = gather(mine, exchanges(mine, (mask,)))
        mine = halves(total, total.shape[0] - 2 * heads)
    other = exchange(mine, far[-1])
    weight_grads, slice_grad, temp_grad = call(
        finish_kernel,
        [
            ((2, owner_rows, width), F32),
            ((head, slices), F32),
            ((1, heads), F32),
        ],
        0,
        2,
    )(mine, other)
    return x_grad, weight_grads, slice_grad, temp_grad.reshape(heads), token_grads


def solution(mesh):
    return jax.shard_map(
        local,
        mesh=mesh,
        in_specs=(P(ALL, None), P(ALL, None), P(), P(), P(), P(), P(), P()),
        out_specs=(P(ALL, None), P(None, "grp", None), P(), P(), P()),
        check_vma=False,
    )
```

```python
import math

import jax
import jax.numpy as jnp
from jax import lax
from jax.experimental import pallas as pl
from jax.experimental.pallas import tpu as pltpu
from jax.sharding import PartitionSpec as P

F32 = jnp.float32
BF16 = jnp.bfloat16
ALL = ("pts", "grp")
LANES = 128
VMEM_LIMIT = 48 * 1024 * 1024
POINTS_LIMIT = 60 * 1024 * 1024


def dot(a, b):
    return lax.dot_general(a, b, (((1,), (0,)), ((), ())), preferred_element_type=F32)


def dot_nt(a, b):
    return lax.dot_general(a, b, (((1,), (1,)), ((), ())), preferred_element_type=F32)


def dot_tn(a, b):
    return lax.dot_general(a, b, (((0,), (0,)), ((), ())), preferred_element_type=F32)


def split(a):
    high = a.astype(BF16)
    return high, (a - high.astype(F32)).astype(BF16)


def dot3(product, a, b):
    return product(a[0], b[0]) + (product(a[1], b[0]) + product(a[0], b[1]))


def head_mask(shape, row_size, lane_size):
    rows = lax.broadcasted_iota(jnp.int32, shape, 0) // row_size
    lanes = lax.broadcasted_iota(jnp.int32, shape, 1) // lane_size
    return rows == lanes


def inverse_row(scalar_ref, index, length):
    return 1.0 / jnp.full((1, length), scalar_ref[index], F32)


def assign(sharp, x, entry, cluster, valid, xmt, weights, live_probs):
    points, width = x.shape
    heads = sharp.shape[0]
    head = width // heads
    slices = cluster.shape[1]
    xm = dot(x[...], entry[...]).astype(BF16)
    xmt[...] = xm.T
    cluster_t = cluster[...].T
    live = (lax.broadcasted_iota(jnp.int32, (1, points), 1) < valid).astype(F32)
    for h in range(heads):
        raw = dot(cluster_t, xmt[h * head : (h + 1) * head, :])
        logits = raw * inverse_row(sharp, h, points)
        e = jnp.exp(logits - jnp.max(logits, axis=0, keepdims=True))
        probs = e * (live / jnp.sum(e, axis=0, keepdims=True))
        if live_probs is not None:
            live_probs[h * slices : (h + 1) * slices, :] = probs
        weights[h * slices : (h + 1) * slices, :] = probs.astype(BF16)
    return xm


def valid_points(tally):
    return tally[lax.axis_index("pts") * lax.axis_size("grp") + lax.axis_index("grp")]


def points_kernel(
    tally_in,
    sharp_in,
    x_in,
    rc_in,
    entry_in,
    exit_in,
    cluster_in,
    payload,
    tally,
    sharp,
    x,
    rc,
    entry,
    exit_,
    cluster,
    xmt,
    weights,
    arrived,
):
    pairs = [
        (entry_in, entry),
        (x_in, x),
        (cluster_in, cluster),
        (sharp_in, sharp),
        (tally_in, tally),
        (exit_in, exit_),
        (rc_in, rc),
    ]
    copies = [
        pltpu.make_async_copy(source, target, arrived.at[i])
        for i, (source, target) in enumerate(pairs)
    ]
    for copy in copies:
        copy.start()
    points, width = x.shape
    heads = sharp.shape[0]
    head = width // heads
    slices = cluster.shape[1]
    per = LANES // head
    groups = heads // per
    for copy in copies:
        copy.wait()
    go = dot_nt(rc[...], exit_[...]).astype(BF16)
    xm = assign(sharp, x, entry, cluster, valid_points(tally), xmt, weights, None)
    rows = groups * slices
    lane_head = lax.broadcasted_iota(jnp.int32, (slices, 2 * LANES), 1) % LANES // head
    for g in range(groups):
        w = weights[g * per * slices : (g + 1) * per * slices, :]
        cut = slice(g * LANES, (g + 1) * LANES)
        full = dot(w, jnp.concatenate([xm[:, cut], go[:, cut]], axis=1))
        own = jnp.zeros((slices, 2 * LANES), F32)
        for j in range(per):
            own = jnp.where(lane_head == j, full[j * slices : (j + 1) * slices, :], own)
        payload[g * slices : (g + 1) * slices, :] = own[:, :LANES].astype(BF16)
        payload[rows + g * slices : rows + (g + 1) * slices, :] = own[:, LANES:].astype(BF16)
    ones = jnp.ones((heads, points), BF16)
    den = jnp.zeros((heads, rows), F32)
    head_row = lax.broadcasted_iota(jnp.int32, (heads, rows), 0)
    lane_group = lax.broadcasted_iota(jnp.int32, (heads, rows), 1) // slices
    for j in range(per):
        w = jnp.concatenate(
            [
                weights[(g * per + j) * slices : (g * per + j + 1) * slices, :]
                for g in range(groups)
            ],
            axis=0,
        )
        den = jnp.where(head_row == lane_group * per + j, dot_nt(ones, w), den)
    high = den.astype(BF16).astype(F32)
    payload[2 * rows :, :] = jnp.concatenate([high, den - high], axis=0).astype(BF16)


def shadow_kernel(
    tally,
    sharp,
    x,
    rc,
    entry,
    exit_,
    cluster,
    maps,
    payload_in,
    payload,
    xmt,
    got,
    weights,
    live_probs,
    maps_high,
    maps_low,
    cluster_rows,
):
    payload[...] = payload_in[...]
    assign(sharp, x, entry, cluster, valid_points(tally), xmt, weights, live_probs)
    got[...] = dot_nt(rc[...], exit_[...]).astype(BF16).T
    head = maps.shape[1]
    slices = cluster.shape[1]
    per = LANES // head
    mask = head_mask((LANES, LANES), head, head)
    for i in range(maps.shape[0]):
        a = jnp.concatenate([maps[i]] * per, axis=0)
        a = jnp.where(mask, jnp.concatenate([a] * per, axis=1), 0.0)
        high, low = split(a)
        maps_high[:, i * LANES : (i + 1) * LANES] = high
        maps_low[:, i * LANES : (i + 1) * LANES] = low
    c = cluster[...].astype(F32).T
    c = jnp.concatenate([c] * per, axis=1)
    c = jnp.concatenate([c] * per, axis=0)
    c = jnp.where(head_mask(c.shape, slices, head), c, 0.0)
    cluster_rows[...] = c.astype(BF16)


def middle_kernel(
    sharp,
    mine,
    other,
    maps_high,
    maps_low,
    cluster_rows,
    xmt,
    got,
    weights,
    live_probs,
    x,
    rc,
    keep,
    send,
    gxmt,
    tokens_out,
    grads_out,
    grad_rows,
):
    points, width = x.shape
    heads = sharp.shape[0]
    head = width // heads
    per = LANES // head
    groups = heads // per
    slices = cluster_rows.shape[0] // per
    rows = groups * slices
    scale = head**-0.5
    total = mine[...].astype(F32) + other[...].astype(F32)
    num = total[:rows]
    mixed_cotangent = total[rows : 2 * rows]
    den_rows = total[2 * rows : 2 * rows + heads] + total[2 * rows + heads : 2 * rows + 2 * heads]
    spread = (
        lax.broadcasted_iota(jnp.int32, (heads, LANES), 0) % per
        == lax.broadcasted_iota(jnp.int32, (heads, LANES), 1) // head
    ).astype(F32)
    d0 = den_rows.astype(BF16)
    rest = den_rows - d0.astype(F32)
    d1 = rest.astype(BF16)
    d2 = (rest - d1.astype(F32)).astype(BF16)
    spread = spread.astype(BF16)
    den = dot_tn(
        jnp.concatenate([d0.astype(F32), d1.astype(F32), d2.astype(F32)], axis=0).astype(BF16),
        jnp.concatenate([spread.astype(F32)] * 3, axis=0).astype(BF16),
    )
    clip_inverse = 1.0 / jnp.maximum(den, 1.0)
    tokens = num * clip_inverse
    tokens_out[...] = tokens
    maps = (maps_high[...], maps_low[...])
    qkv = dot3(dot, split(tokens), maps)
    wide = (LANES, per * slices)
    lane_mask = head_mask(wide, head, slices)
    row_mask = head_mask((per * slices, LANES), slices, head)

    def spread_heads(a):
        doubled = jnp.concatenate([a] * (LANES // slices), axis=0).T
        doubled = jnp.concatenate([doubled] * (per * slices // LANES), axis=1)
        return split(jnp.where(lane_mask, doubled, 0.0))

    def fold_heads(a):
        kept = jnp.where(row_mask, a, 0.0)
        out = kept[:slices]
        for j in range(1, per):
            out = out + kept[j * slices : (j + 1) * slices]
        return kept, out

    mixed_blocks, query_grads, key_grads, value_grads = [], [], [], []
    for g in range(groups):
        cut = slice(g * slices, (g + 1) * slices)
        q, k, v = (qkv[cut, i * LANES : (i + 1) * LANES] for i in range(3))
        gm = mixed_cotangent[cut]
        q_blocks, gm_blocks = spread_heads(q), spread_heads(gm)
        k2, v2 = split(k), split(v)
        scores = dot3(dot, k2, q_blocks) * scale
        g_attn = dot3(dot, v2, gm_blocks)
        e = jnp.exp(scores - jnp.max(scores, axis=0, keepdims=True))
        attn = e / jnp.sum(e, axis=0, keepdims=True)
        g_scores = attn * (g_attn - jnp.sum(g_attn * attn, axis=0, keepdims=True)) * scale
        attn2, gs2 = split(attn), split(g_scores)
        value_grads.append(dot3(dot_nt, attn2, gm_blocks))
        key_grads.append(dot3(dot_nt, gs2, q_blocks))
        attn_t, gs_t = split(attn.T), split(g_scores.T)
        query_grads.append(fold_heads(dot3(dot, gs_t, k2))[1])
        mixed_blocks.append(fold_heads(dot3(dot, attn_t, v2))[0].astype(BF16))
    grads = jnp.concatenate(
        [
            jnp.concatenate(query_grads, axis=0),
            jnp.concatenate(key_grads, axis=0),
            jnp.concatenate(value_grads, axis=0),
        ],
        axis=1,
    )
    grads_out[...] = grads
    token_cotangent = dot3(dot_nt, split(grads), maps)
    num_cotangent = token_cotangent * clip_inverse
    den_terms = jnp.where(den > 1.0, -token_cotangent * tokens * clip_inverse, 0.0)

    owners = grad_rows.shape[0]
    owner_rows = width // owners
    slice_sum = jnp.zeros((head, per * slices), F32)
    slice_mask = head_mask((LANES, per * slices), head, slices)
    temps = []
    for g in range(groups):
        cut = slice(g * slices, (g + 1) * slices)
        big = slice(g * per * slices, (g + 1) * per * slices)
        small = slice(g * LANES, (g + 1) * LANES)
        num_block = jnp.where(
            row_mask, jnp.concatenate([num_cotangent[cut]] * per, axis=0), 0.0
        ).astype(BF16)
        den_column = jnp.sum(
            jnp.where(row_mask, jnp.concatenate([den_terms[cut]] * per, axis=0), 0.0),
            axis=1,
            keepdims=True,
        )
        table = jnp.concatenate([mixed_blocks[g], num_block], axis=1)
        w = weights[big, :]
        xm_g = xmt[small, :]
        both = dot_tn(table, w)
        merged = both[:LANES].astype(BF16)
        grad_exit = dot(merged, rc[...])
        g_w = dot(table, jnp.concatenate([got[small, :], xm_g], axis=0)) + den_column
        raw = dot(cluster_rows[...], xm_g)
        g_raw = []
        for j in range(per):
            h = g * per + j
            part = slice(j * slices, (j + 1) * slices)
            lp = live_probs[h * slices : (h + 1) * slices, :]
            t = g_w[part] * lp
            g_logits = t - lp * jnp.sum(t, axis=0, keepdims=True)
            inverse = inverse_row(sharp, h, points)
            row = jnp.sum(g_logits * raw[part], axis=0, keepdims=True) * (inverse * inverse)
            temps.append(-row)
            g_raw.append((g_logits * inverse).astype(BF16))
        g_raw = jnp.concatenate(g_raw, axis=0)
        g_xm = (both[LANES:] + dot_tn(cluster_rows[...], g_raw)).astype(BF16)
        gxmt[small, :] = g_xm
        grad_entry = dot(g_xm, x[...]).T
        block = jnp.where(slice_mask, dot_nt(xm_g, g_raw), 0.0)
        for j in range(per):
            slice_sum = slice_sum + block[j * head : (j + 1) * head]
        for o in range(owners):
            grad_rows[o, :owner_rows, small] = grad_entry[
                o * owner_rows : (o + 1) * owner_rows
            ].astype(BF16)
        for r in range(g * LANES // owner_rows, (g + 1) * LANES // owner_rows):
            start = r * owner_rows - g * LANES
            grad_rows[r, owner_rows:, :] = grad_exit[start : start + owner_rows].astype(BF16)
    folded = slice_sum[:, :LANES]
    for i in range(1, per * slices // LANES):
        folded = folded + slice_sum[:, i * LANES : (i + 1) * LANES]
    folded = folded + pltpu.roll(folded, LANES // 2, 1)
    part = head * slices // width
    low = lax.broadcasted_iota(jnp.int32, (part, LANES), 1) < slices
    slice_rows = [
        jnp.where(low, folded[i * part : (i + 1) * part], folded[(i + 1) * part : (i + 2) * part])
        for i in range(0, head // part, 2)
    ]
    temp = jnp.sum(jnp.concatenate(temps, axis=0), axis=1, keepdims=True)
    temp = jnp.broadcast_to(temp, (heads, width // 2))
    temp_high = temp.astype(BF16).astype(F32)
    extra = jnp.concatenate(
        [
            jnp.concatenate(slice_rows, axis=1),
            jnp.concatenate([temp_high, temp - temp_high], axis=1),
        ],
        axis=0,
    ).astype(BF16)
    odd = lax.axis_index("grp") % 2
    chunk = 2 * owner_rows
    for i in range(owners // 2):
        keep[i * chunk : (i + 1) * chunk, :] = grad_rows[2 * i + odd]
        send[i * chunk : (i + 1) * chunk, :] = grad_rows[2 * i + 1 - odd]
    keep[owners // 2 * chunk :, :] = extra
    send[owners // 2 * chunk :, :] = extra


def features_kernel(gxmt, entry, tokens, grads, x_grad, token_grads):
    x_grad[...] = dot_nt(gxmt[...].T, entry[...]).astype(BF16)
    maps, head = token_grads.shape[:2]
    per = LANES // head
    full = dot3(dot, split(tokens[...].T), split(grads[...]))
    for i in range(maps):
        part = full[:, i * LANES : (i + 1) * LANES]
        part = jnp.where(head_mask((LANES, LANES), head, head), part, 0.0)
        out = part[:head]
        for j in range(1, per):
            out = out + part[j * head : (j + 1) * head]
        shift = LANES // 2
        while shift >= head:
            out = out + pltpu.roll(out, shift, 1)
            shift //= 2
        token_grads[i] = out[:, :head]


def finish_kernel(mine, other, weight_grads, slice_grad, temp_grad):
    total = mine[...].astype(F32) + other[...].astype(F32)
    owner_rows = weight_grads.shape[1]
    head, slices = slice_grad.shape
    weight_grads[0] = total[:owner_rows]
    weight_grads[1] = total[owner_rows : 2 * owner_rows]
    extra = total[2 * owner_rows :]
    part = head * slices // extra.shape[1]
    for i in range(head // part):
        tile = extra[:part, i // 2 * LANES : (i // 2 + 1) * LANES]
        if i % 2:
            tile = pltpu.roll(tile, LANES // 2, 1)
        slice_grad[i * part : (i + 1) * part, :] = tile[:, :slices]
    heads = temp_grad.shape[1]
    temp = extra[part:]
    middle = temp.shape[1] // 2
    temp = (temp[:, :middle] + temp[:, middle:])[:, :LANES]
    temp = jnp.where(head_mask(temp.shape, 1, 1), temp, 0.0)
    temp_grad[...] = jnp.sum(temp, axis=0, keepdims=True)[:, :heads]


def call(kernel, shapes, in_smem, count, scratch=(), space=pltpu.VMEM, limit=VMEM_LIMIT):
    smem = pl.BlockSpec(memory_space=pltpu.SMEM)
    vmem = pl.BlockSpec(memory_space=pltpu.VMEM)
    rest = pl.BlockSpec(memory_space=space)
    return pl.pallas_call(
        kernel,
        out_shape=[jax.ShapeDtypeStruct(s, d) for s, d in shapes],
        in_specs=[smem] * in_smem + [rest] * (count - in_smem),
        out_specs=[vmem] * len(shapes),
        scratch_shapes=list(scratch),
        compiler_params=pltpu.CompilerParams(vmem_limit_bytes=limit),
    )


def exchange(a, mask):
    devices = lax.axis_size("pts") * lax.axis_size("grp")
    return lax.ppermute(a, ALL, [(i, i ^ mask) for i in range(devices)])


def exchanges(a, masks):
    return [exchange(a, mask) for mask in masks]


def gather(mine, others):
    mine, others = mine.astype(F32), [a.astype(F32) for a in others]
    if len(others) == 1:
        return mine + others[0]
    return (mine + others[0]) + (others[1] + others[2])


def token_pack(values, start, root_scale, den_scale):
    sums, pair = values[:start], values[start:]
    n = pair.shape[0] // 2
    pair = (pair[:n] + pair[n:]) * den_scale
    high = lax.reduce_precision(pair, 8, 7)
    roots = jnp.sqrt(jnp.abs(sums)) * root_scale
    roots = jnp.where(sums < 0.0, -roots, roots)
    return jnp.concatenate([roots, high, pair - high], axis=0).astype(jnp.float16)


def token_unpack(packed, start, root_scale, den_scale):
    packed = packed.astype(F32)
    row = lax.broadcasted_iota(jnp.int32, packed.shape, 0)
    return packed * jnp.where(row < start, jnp.abs(packed) * root_scale**-2, 1.0 / den_scale)


def halves(total, start):
    pair = total[start:]
    n = pair.shape[1] // 2
    pair = pair[:, :n] + pair[:, n:]
    high = lax.reduce_precision(pair, 8, 7)
    pair = jnp.concatenate([high, pair - high], axis=1)
    return jnp.concatenate([total[:start], pair], axis=0).astype(BF16)


def local(x, rc, entry, exit_, cluster, sharp, maps, tally):
    points, width = x.shape
    heads = sharp.shape[0]
    head, slices = cluster.shape
    owners = lax.axis_size("grp")
    devices = lax.axis_size("pts") * owners
    per = LANES // head
    rows = heads // per * slices
    token_rows = 2 * rows + 2 * heads
    far = [1 << bit for bit in range(4, devices.bit_length() - 1)]
    (payload,) = call(
        points_kernel,
        [((token_rows, LANES), BF16)],
        0,
        7,
        scratch=[
            pltpu.SMEM(tally.shape, tally.dtype),
            pltpu.SMEM(sharp.shape, sharp.dtype),
            *(pltpu.VMEM(a.shape, a.dtype) for a in (x, rc, entry, exit_, cluster)),
            pltpu.VMEM((width, points), BF16),
            pltpu.VMEM((heads * slices, points), BF16),
            pltpu.SemaphoreType.DMA((7,)),
        ],
        space=pltpu.HBM,
        limit=POINTS_LIMIT,
    )(tally, sharp, x, rc, entry, exit_, cluster)
    steps = ((8,), *((mask,) for mask in far), (2, 4, 6), (1,))
    all_points = devices * points
    root_scale = 2.0 ** math.floor(math.log2(65000.0 / math.sqrt(all_points * width * 2.25)))
    den_scale = 2.0 ** -max(0, math.ceil(math.log2(all_points / 2.0**15)))
    others = exchanges(payload, steps[0])
    mine, xmt, got, weights, live_probs, maps_high, maps_low, cluster_rows = call(
        shadow_kernel,
        [
            ((token_rows, LANES), BF16),
            ((width, points), BF16),
            ((width, points), BF16),
            ((heads * slices, points), BF16),
            ((heads * slices, points), F32),
            ((LANES, 3 * LANES), BF16),
            ((LANES, 3 * LANES), BF16),
            ((per * slices, LANES), BF16),
        ],
        2,
        9,
    )(tally, sharp, x, rc, entry, exit_, cluster, maps, payload)
    total = gather(mine, others)
    for masks in steps[1:-1]:
        mine = token_pack(total, 2 * rows, root_scale, den_scale)
        others = exchanges(mine, masks)
        mine, *others = (
            token_unpack(a, 2 * rows, root_scale, den_scale) for a in (mine, *others)
        )
        total = gather(mine, others)
    mine = total
    (other,) = exchanges(mine, steps[-1])

    owner_rows = width // owners
    chunk = 2 * owner_rows
    extra = head * slices // width + heads
    keep, send, gxmt, tokens, grads = call(
        middle_kernel,
        [
            ((owners // 2 * chunk + extra, width), BF16),
            ((owners // 2 * chunk + extra, width), BF16),
            ((width, points), BF16),
            ((rows, LANES), F32),
            ((rows, 3 * LANES), F32),
        ],
        1,
        12,
        scratch=[pltpu.VMEM((owners, chunk, width), BF16)],
    )(
        sharp,
        mine,
        other,
        maps_high,
        maps_low,
        cluster_rows,
        xmt,
        got,
        weights,
        live_probs,
        x,
        rc,
    )

    got_half = exchange(send, 1)
    x_grad, token_grads = call(
        features_kernel,
        [((points, width), BF16), (maps.shape, F32)],
        0,
        4,
    )(gxmt, entry, tokens, grads)
    total = keep.astype(F32) + got_half.astype(F32)
    total = halves(total, total.shape[0] - heads)
    half = lax.axis_index("grp") // 2
    common = total[owners // 2 * chunk :]
    mine = jnp.concatenate(
        [lax.dynamic_slice_in_dim(total, half * chunk, chunk), common], axis=0
    )
    theirs = jnp.concatenate(
        [lax.dynamic_slice_in_dim(total, (1 - half) * chunk, chunk), common], axis=0
    )
    others = [exchange(mine, 4), exchange(theirs, 2), exchange(theirs, 6)]
    total = gather(mine, others)
    mine = halves(total, total.shape[0] - heads)
    for mask in (8, *far[:-1]):
        total = gather(mine, exchanges(mine, (mask,)))
        mine = halves(total, total.shape[0] - heads)
    other = exchange(mine, far[-1])
    weight_grads, slice_grad, temp_grad = call(
        finish_kernel,
        [
            ((2, owner_rows, width), F32),
            ((head, slices), F32),
            ((1, heads), F32),
        ],
        0,
        2,
    )(mine, other)
    return x_grad, weight_grads, slice_grad, temp_grad.reshape(heads), token_grads


def solution(mesh):
    return jax.shard_map(
        local,
        mesh=mesh,
        in_specs=(P(ALL, None), P(ALL, None), P(), P(), P(), P(), P(), P()),
        out_specs=(P(ALL, None), P(None, "grp", None), P(), P(), P()),
        check_vma=False,
    )
```

```python
import math

import jax
import jax.numpy as jnp
from jax import lax
from jax.experimental import pallas as pl
from jax.experimental.pallas import tpu as pltpu
from jax.sharding import PartitionSpec as P

F32 = jnp.float32
BF16 = jnp.bfloat16
ALL = ("pts", "grp")
LANES = 128
VMEM_LIMIT = 48 * 1024 * 1024
OPENING_FLOPS = 3_000_000_000


def dot(a, b):
    return lax.dot_general(a, b, (((1,), (0,)), ((), ())), preferred_element_type=F32)


def dot_nt(a, b):
    return lax.dot_general(a, b, (((1,), (1,)), ((), ())), preferred_element_type=F32)


def dot_tn(a, b):
    return lax.dot_general(a, b, (((0,), (0,)), ((), ())), preferred_element_type=F32)


def split(a):
    high = a.astype(BF16)
    return high, (a - high.astype(F32)).astype(BF16)


def dot3(product, a, b):
    return product(a[0], b[0]) + (product(a[1], b[0]) + product(a[0], b[1]))


def head_mask(shape, row_size, lane_size):
    rows = lax.broadcasted_iota(jnp.int32, shape, 0) // row_size
    lanes = lax.broadcasted_iota(jnp.int32, shape, 1) // lane_size
    return rows == lanes


def inverse_row(scalar_ref, index, length):
    return 1.0 / jnp.full((1, length), scalar_ref[index], F32)


def assign(sharp, x, entry, cluster, valid, xmt, weights, live_probs):
    points, width = x.shape
    heads = sharp.shape[0]
    head = width // heads
    slices = cluster.shape[1]
    xm = dot(x[...], entry[...]).astype(BF16)
    xmt[...] = xm.T
    cluster_t = cluster[...].T
    live = (lax.broadcasted_iota(jnp.int32, (1, points), 1) < valid).astype(F32)
    for h in range(heads):
        raw = dot(cluster_t, xmt[h * head : (h + 1) * head, :])
        logits = raw * inverse_row(sharp, h, points)
        e = jnp.exp(logits - jnp.max(logits, axis=0, keepdims=True))
        probs = e * (live / jnp.sum(e, axis=0, keepdims=True))
        if live_probs is not None:
            live_probs[h * slices : (h + 1) * slices, :] = probs
        weights[h * slices : (h + 1) * slices, :] = probs.astype(BF16)
    return xm


def valid_points(tally):
    return tally[lax.axis_index("pts") * lax.axis_size("grp") + lax.axis_index("grp")]


def opening_kernel(out):
    out[...] = jnp.zeros_like(out)


def points_kernel(
    tally, sharp, x, rc, entry, exit_, cluster, opening, payload, xmt, weights
):
    points, width = x.shape
    heads = sharp.shape[0]
    head = width // heads
    slices = cluster.shape[1]
    per = LANES // head
    groups = heads // per
    go = dot_nt(rc[...], exit_[...]).astype(BF16)
    xm = assign(sharp, x, entry, cluster, valid_points(tally), xmt, weights, None)
    rows = groups * slices
    lane_head = lax.broadcasted_iota(jnp.int32, (slices, 2 * LANES), 1) % LANES // head
    for g in range(groups):
        w = weights[g * per * slices : (g + 1) * per * slices, :]
        cut = slice(g * LANES, (g + 1) * LANES)
        full = dot(w, jnp.concatenate([xm[:, cut], go[:, cut]], axis=1))
        own = jnp.zeros((slices, 2 * LANES), F32)
        for j in range(per):
            own = jnp.where(lane_head == j, full[j * slices : (j + 1) * slices, :], own)
        payload[g * slices : (g + 1) * slices, :] = own[:, :LANES].astype(BF16)
        payload[rows + g * slices : rows + (g + 1) * slices, :] = own[:, LANES:].astype(BF16)
    ones = jnp.ones((heads, points), BF16)
    den = jnp.zeros((heads, rows), F32)
    head_row = lax.broadcasted_iota(jnp.int32, (heads, rows), 0)
    lane_group = lax.broadcasted_iota(jnp.int32, (heads, rows), 1) // slices
    for j in range(per):
        w = jnp.concatenate(
            [
                weights[(g * per + j) * slices : (g * per + j + 1) * slices, :]
                for g in range(groups)
            ],
            axis=0,
        )
        den = jnp.where(head_row == lane_group * per + j, dot_nt(ones, w), den)
    high = den.astype(BF16).astype(F32)
    payload[2 * rows :, :] = jnp.concatenate([high, den - high], axis=0).astype(BF16)


def shadow_kernel(
    tally,
    sharp,
    x,
    rc,
    entry,
    exit_,
    cluster,
    maps,
    payload_in,
    payload,
    xmt,
    got,
    weights,
    live_probs,
    maps_high,
    maps_low,
    cluster_rows,
):
    payload[...] = payload_in[...]
    assign(sharp, x, entry, cluster, valid_points(tally), xmt, weights, live_probs)
    got[...] = dot_nt(rc[...], exit_[...]).astype(BF16).T
    head = maps.shape[1]
    slices = cluster.shape[1]
    per = LANES // head
    mask = head_mask((LANES, LANES), head, head)
    for i in range(maps.shape[0]):
        a = jnp.concatenate([maps[i]] * per, axis=0)
        a = jnp.where(mask, jnp.concatenate([a] * per, axis=1), 0.0)
        high, low = split(a)
        maps_high[:, i * LANES : (i + 1) * LANES] = high
        maps_low[:, i * LANES : (i + 1) * LANES] = low
    c = cluster[...].astype(F32).T
    c = jnp.concatenate([c] * per, axis=1)
    c = jnp.concatenate([c] * per, axis=0)
    c = jnp.where(head_mask(c.shape, slices, head), c, 0.0)
    cluster_rows[...] = c.astype(BF16)


def middle_kernel(
    sharp,
    mine,
    other,
    maps_high,
    maps_low,
    cluster_rows,
    xmt,
    got,
    weights,
    live_probs,
    x,
    rc,
    keep,
    send,
    gxmt,
    tokens_out,
    grads_out,
    grad_rows,
):
    points, width = x.shape
    heads = sharp.shape[0]
    head = width // heads
    per = LANES // head
    groups = heads // per
    slices = cluster_rows.shape[0] // per
    rows = groups * slices
    scale = head**-0.5
    total = mine[...].astype(F32) + other[...].astype(F32)
    num = total[:rows]
    mixed_cotangent = total[rows : 2 * rows]
    den_rows = total[2 * rows : 2 * rows + heads] + total[2 * rows + heads : 2 * rows + 2 * heads]
    spread = (
        lax.broadcasted_iota(jnp.int32, (heads, LANES), 0) % per
        == lax.broadcasted_iota(jnp.int32, (heads, LANES), 1) // head
    ).astype(F32)
    d0 = den_rows.astype(BF16)
    rest = den_rows - d0.astype(F32)
    d1 = rest.astype(BF16)
    d2 = (rest - d1.astype(F32)).astype(BF16)
    spread = spread.astype(BF16)
    den = dot_tn(
        jnp.concatenate([d0.astype(F32), d1.astype(F32), d2.astype(F32)], axis=0).astype(BF16),
        jnp.concatenate([spread.astype(F32)] * 3, axis=0).astype(BF16),
    )
    clip_inverse = 1.0 / jnp.maximum(den, 1.0)
    tokens = num * clip_inverse
    tokens_out[...] = tokens
    maps = (maps_high[...], maps_low[...])
    qkv = dot3(dot, split(tokens), maps)
    wide = (LANES, per * slices)
    lane_mask = head_mask(wide, head, slices)
    row_mask = head_mask((per * slices, LANES), slices, head)

    def spread_heads(a):
        doubled = jnp.concatenate([a] * (LANES // slices), axis=0).T
        doubled = jnp.concatenate([doubled] * (per * slices // LANES), axis=1)
        return split(jnp.where(lane_mask, doubled, 0.0))

    def fold_heads(a):
        kept = jnp.where(row_mask, a, 0.0)
        out = kept[:slices]
        for j in range(1, per):
            out = out + kept[j * slices : (j + 1) * slices]
        return kept, out

    mixed_blocks, query_grads, key_grads, value_grads = [], [], [], []
    for g in range(groups):
        cut = slice(g * slices, (g + 1) * slices)
        q, k, v = (qkv[cut, i * LANES : (i + 1) * LANES] for i in range(3))
        gm = mixed_cotangent[cut]
        q_blocks, gm_blocks = spread_heads(q), spread_heads(gm)
        k2, v2 = split(k), split(v)
        scores = dot3(dot, k2, q_blocks) * scale
        g_attn = dot3(dot, v2, gm_blocks)
        e = jnp.exp(scores - jnp.max(scores, axis=0, keepdims=True))
        attn = e / jnp.sum(e, axis=0, keepdims=True)
        g_scores = attn * (g_attn - jnp.sum(g_attn * attn, axis=0, keepdims=True)) * scale
        attn2, gs2 = split(attn), split(g_scores)
        value_grads.append(dot3(dot_nt, attn2, gm_blocks))
        key_grads.append(dot3(dot_nt, gs2, q_blocks))
        attn_t, gs_t = split(attn.T), split(g_scores.T)
        query_grads.append(fold_heads(dot3(dot, gs_t, k2))[1])
        mixed_blocks.append(fold_heads(dot3(dot, attn_t, v2))[0].astype(BF16))
    grads = jnp.concatenate(
        [
            jnp.concatenate(query_grads, axis=0),
            jnp.concatenate(key_grads, axis=0),
            jnp.concatenate(value_grads, axis=0),
        ],
        axis=1,
    )
    grads_out[...] = grads
    token_cotangent = dot3(dot_nt, split(grads), maps)
    num_cotangent = token_cotangent * clip_inverse
    den_terms = jnp.where(den > 1.0, -token_cotangent * tokens * clip_inverse, 0.0)

    owners = grad_rows.shape[0]
    owner_rows = width // owners
    slice_sum = jnp.zeros((head, per * slices), F32)
    slice_mask = head_mask((LANES, per * slices), head, slices)
    temps = []
    for g in range(groups):
        cut = slice(g * slices, (g + 1) * slices)
        big = slice(g * per * slices, (g + 1) * per * slices)
        small = slice(g * LANES, (g + 1) * LANES)
        num_block = jnp.where(
            row_mask, jnp.concatenate([num_cotangent[cut]] * per, axis=0), 0.0
        ).astype(BF16)
        den_column = jnp.sum(
            jnp.where(row_mask, jnp.concatenate([den_terms[cut]] * per, axis=0), 0.0),
            axis=1,
            keepdims=True,
        )
        table = jnp.concatenate([mixed_blocks[g], num_block], axis=1)
        w = weights[big, :]
        xm_g = xmt[small, :]
        both = dot_tn(table, w)
        merged = both[:LANES].astype(BF16)
        grad_exit = dot(merged, rc[...])
        g_w = dot(table, jnp.concatenate([got[small, :], xm_g], axis=0)) + den_column
        raw = dot(cluster_rows[...], xm_g)
        g_raw = []
        for j in range(per):
            h = g * per + j
            part = slice(j * slices, (j + 1) * slices)
            lp = live_probs[h * slices : (h + 1) * slices, :]
            t = g_w[part] * lp
            g_logits = t - lp * jnp.sum(t, axis=0, keepdims=True)
            inverse = inverse_row(sharp, h, points)
            row = jnp.sum(g_logits * raw[part], axis=0, keepdims=True) * (inverse * inverse)
            temps.append(-row)
            g_raw.append((g_logits * inverse).astype(BF16))
        g_raw = jnp.concatenate(g_raw, axis=0)
        g_xm = (both[LANES:] + dot_tn(cluster_rows[...], g_raw)).astype(BF16)
        gxmt[small, :] = g_xm
        grad_entry = dot(g_xm, x[...]).T
        block = jnp.where(slice_mask, dot_nt(xm_g, g_raw), 0.0)
        for j in range(per):
            slice_sum = slice_sum + block[j * head : (j + 1) * head]
        for o in range(owners):
            grad_rows[o, :owner_rows, small] = grad_entry[
                o * owner_rows : (o + 1) * owner_rows
            ].astype(BF16)
        for r in range(g * LANES // owner_rows, (g + 1) * LANES // owner_rows):
            start = r * owner_rows - g * LANES
            grad_rows[r, owner_rows:, :] = grad_exit[start : start + owner_rows].astype(BF16)
    folded = slice_sum[:, :LANES]
    for i in range(1, per * slices // LANES):
        folded = folded + slice_sum[:, i * LANES : (i + 1) * LANES]
    folded = folded + pltpu.roll(folded, LANES // 2, 1)
    part = head * slices // width
    low = lax.broadcasted_iota(jnp.int32, (part, LANES), 1) < slices
    slice_rows = [
        jnp.where(low, folded[i * part : (i + 1) * part], folded[(i + 1) * part : (i + 2) * part])
        for i in range(0, head // part, 2)
    ]
    temp = jnp.sum(jnp.concatenate(temps, axis=0), axis=1, keepdims=True)
    temp = jnp.broadcast_to(temp, (heads, width // 2))
    temp_high = temp.astype(BF16).astype(F32)
    extra = jnp.concatenate(
        [
            jnp.concatenate(slice_rows, axis=1),
            jnp.concatenate([temp_high, temp - temp_high], axis=1),
        ],
        axis=0,
    ).astype(BF16)
    odd = lax.axis_index("grp") % 2
    chunk = 2 * owner_rows
    for i in range(owners // 2):
        keep[i * chunk : (i + 1) * chunk, :] = grad_rows[2 * i + odd]
        send[i * chunk : (i + 1) * chunk, :] = grad_rows[2 * i + 1 - odd]
    keep[owners // 2 * chunk :, :] = extra
    send[owners // 2 * chunk :, :] = extra


def features_kernel(gxmt, entry, tokens, grads, x_grad, token_grads):
    x_grad[...] = dot_nt(gxmt[...].T, entry[...]).astype(BF16)
    maps, head = token_grads.shape[:2]
    per = LANES // head
    full = dot3(dot, split(tokens[...].T), split(grads[...]))
    for i in range(maps):
        part = full[:, i * LANES : (i + 1) * LANES]
        part = jnp.where(head_mask((LANES, LANES), head, head), part, 0.0)
        out = part[:head]
        for j in range(1, per):
            out = out + part[j * head : (j + 1) * head]
        shift = LANES // 2
        while shift >= head:
            out = out + pltpu.roll(out, shift, 1)
            shift //= 2
        token_grads[i] = out[:, :head]


def finish_kernel(mine, other, weight_grads, slice_grad, temp_grad):
    total = mine[...].astype(F32) + other[...].astype(F32)
    owner_rows = weight_grads.shape[1]
    head, slices = slice_grad.shape
    weight_grads[0] = total[:owner_rows]
    weight_grads[1] = total[owner_rows : 2 * owner_rows]
    extra = total[2 * owner_rows :]
    part = head * slices // extra.shape[1]
    for i in range(head // part):
        tile = extra[:part, i // 2 * LANES : (i // 2 + 1) * LANES]
        if i % 2:
            tile = pltpu.roll(tile, LANES // 2, 1)
        slice_grad[i * part : (i + 1) * part, :] = tile[:, :slices]
    heads = temp_grad.shape[1]
    temp = extra[part:]
    middle = temp.shape[1] // 2
    temp = (temp[:, :middle] + temp[:, middle:])[:, :LANES]
    temp = jnp.where(head_mask(temp.shape, 1, 1), temp, 0.0)
    temp_grad[...] = jnp.sum(temp, axis=0, keepdims=True)[:, :heads]


def call(kernel, shapes, in_smem, count, scratch=(), space=pltpu.VMEM, limit=VMEM_LIMIT, flops=0):
    smem = pl.BlockSpec(memory_space=pltpu.SMEM)
    vmem = pl.BlockSpec(memory_space=pltpu.VMEM)
    rest = pl.BlockSpec(memory_space=space)
    return pl.pallas_call(
        kernel,
        out_shape=[jax.ShapeDtypeStruct(s, d) for s, d in shapes],
        in_specs=[smem] * in_smem + [rest] * (count - in_smem),
        out_specs=[vmem] * len(shapes),
        scratch_shapes=list(scratch),
        compiler_params=pltpu.CompilerParams(vmem_limit_bytes=limit),
        cost_estimate=pl.CostEstimate(flops=flops, bytes_accessed=0, transcendentals=0)
        if flops
        else None,
    )


def exchange(a, mask):
    devices = lax.axis_size("pts") * lax.axis_size("grp")
    return lax.ppermute(a, ALL, [(i, i ^ mask) for i in range(devices)])


def exchanges(a, masks):
    return [exchange(a, mask) for mask in masks]


def gather(mine, others):
    mine, others = mine.astype(F32), [a.astype(F32) for a in others]
    if len(others) == 1:
        return mine + others[0]
    return (mine + others[0]) + (others[1] + others[2])


def token_pack(values, start, root_scale, den_scale):
    sums, pair = values[:start], values[start:]
    n = pair.shape[0] // 2
    pair = (pair[:n] + pair[n:]) * den_scale
    high = lax.reduce_precision(pair, 8, 7)
    roots = jnp.sqrt(jnp.abs(sums)) * root_scale
    roots = jnp.where(sums < 0.0, -roots, roots)
    return jnp.concatenate([roots, high, pair - high], axis=0).astype(jnp.float16)


def token_unpack(packed, start, root_scale, den_scale):
    packed = packed.astype(F32)
    row = lax.broadcasted_iota(jnp.int32, packed.shape, 0)
    return packed * jnp.where(row < start, jnp.abs(packed) * root_scale**-2, 1.0 / den_scale)


def halves(total, start):
    pair = total[start:]
    n = pair.shape[1] // 2
    pair = pair[:, :n] + pair[:, n:]
    high = lax.reduce_precision(pair, 8, 7)
    pair = jnp.concatenate([high, pair - high], axis=1)
    return jnp.concatenate([total[:start], pair], axis=0).astype(BF16)


def local(x, rc, entry, exit_, cluster, sharp, maps, tally):
    points, width = x.shape
    heads = sharp.shape[0]
    head, slices = cluster.shape
    owners = lax.axis_size("grp")
    devices = lax.axis_size("pts") * owners
    per = LANES // head
    rows = heads // per * slices
    token_rows = 2 * rows + 2 * heads
    far = [1 << bit for bit in range(4, devices.bit_length() - 1)]
    (opening,) = call(opening_kernel, [((8, LANES), F32)], 0, 0, flops=OPENING_FLOPS)()
    (payload,) = call(
        points_kernel,
        [((token_rows, LANES), BF16)],
        2,
        8,
        scratch=[
            pltpu.VMEM((width, points), BF16),
            pltpu.VMEM((heads * slices, points), BF16),
        ],
    )(tally, sharp, x, rc, entry, exit_, cluster, opening)
    steps = ((8,), *((mask,) for mask in far), (2, 4, 6), (1,))
    all_points = devices * points
    root_scale = 2.0 ** math.floor(math.log2(65000.0 / math.sqrt(all_points * width * 2.25)))
    den_scale = 2.0 ** -max(0, math.ceil(math.log2(all_points / 2.0**15)))
    others = exchanges(payload, steps[0])
    mine, xmt, got, weights, live_probs, maps_high, maps_low, cluster_rows = call(
        shadow_kernel,
        [
            ((token_rows, LANES), BF16),
            ((width, points), BF16),
            ((width, points), BF16),
            ((heads * slices, points), BF16),
            ((heads * slices, points), F32),
            ((LANES, 3 * LANES), BF16),
            ((LANES, 3 * LANES), BF16),
            ((per * slices, LANES), BF16),
        ],
        2,
        9,
    )(tally, sharp, x, rc, entry, exit_, cluster, maps, payload)
    total = gather(mine, others)
    for masks in steps[1:-1]:
        mine = token_pack(total, 2 * rows, root_scale, den_scale)
        others = exchanges(mine, masks)
        mine, *others = (
            token_unpack(a, 2 * rows, root_scale, den_scale) for a in (mine, *others)
        )
        total = gather(mine, others)
    mine = total
    (other,) = exchanges(mine, steps[-1])

    owner_rows = width // owners
    chunk = 2 * owner_rows
    extra = head * slices // width + heads
    keep, send, gxmt, tokens, grads = call(
        middle_kernel,
        [
            ((owners // 2 * chunk + extra, width), BF16),
            ((owners // 2 * chunk + extra, width), BF16),
            ((width, points), BF16),
            ((rows, LANES), F32),
            ((rows, 3 * LANES), F32),
        ],
        1,
        12,
        scratch=[pltpu.VMEM((owners, chunk, width), BF16)],
    )(
        sharp,
        mine,
        other,
        maps_high,
        maps_low,
        cluster_rows,
        xmt,
        got,
        weights,
        live_probs,
        x,
        rc,
    )

    got_half = exchange(send, 1)
    x_grad, token_grads = call(
        features_kernel,
        [((points, width), BF16), (maps.shape, F32)],
        0,
        4,
    )(gxmt, entry, tokens, grads)
    total = keep.astype(F32) + got_half.astype(F32)
    total = halves(total, total.shape[0] - heads)
    half = lax.axis_index("grp") // 2
    common = total[owners // 2 * chunk :]
    mine = jnp.concatenate(
        [lax.dynamic_slice_in_dim(total, half * chunk, chunk), common], axis=0
    )
    theirs = jnp.concatenate(
        [lax.dynamic_slice_in_dim(total, (1 - half) * chunk, chunk), common], axis=0
    )
    others = [exchange(mine, 4), exchange(theirs, 2), exchange(theirs, 6)]
    total = gather(mine, others)
    mine = halves(total, total.shape[0] - heads)
    for mask in (8, *far[:-1]):
        total = gather(mine, exchanges(mine, (mask,)))
        mine = halves(total, total.shape[0] - heads)
    other = exchange(mine, far[-1])
    weight_grads, slice_grad, temp_grad = call(
        finish_kernel,
        [
            ((2, owner_rows, width), F32),
            ((head, slices), F32),
            ((1, heads), F32),
        ],
        0,
        2,
    )(mine, other)
    return x_grad, weight_grads, slice_grad, temp_grad.reshape(heads), token_grads


def solution(mesh):
    return jax.shard_map(
        local,
        mesh=mesh,
        in_specs=(P(ALL, None), P(ALL, None), P(), P(), P(), P(), P(), P()),
        out_specs=(P(ALL, None), P(None, "grp", None), P(), P(), P()),
        check_vma=False,
    )
```

```python
import functools
import math

import jax
import jax.numpy as jnp
from jax import lax
from jax.experimental import pallas as pl
from jax.experimental.pallas import tpu as pltpu
from jax.sharding import PartitionSpec as P

F32 = jnp.float32
BF16 = jnp.bfloat16
ALL = ("pts", "grp")
LANES = 128
VMEM_LIMIT = 48 * 1024 * 1024
OPENING_FLOPS = 3_000_000_000


def dot(a, b):
    return lax.dot_general(a, b, (((1,), (0,)), ((), ())), preferred_element_type=F32)


def dot_nt(a, b):
    return lax.dot_general(a, b, (((1,), (1,)), ((), ())), preferred_element_type=F32)


def dot_tn(a, b):
    return lax.dot_general(a, b, (((0,), (0,)), ((), ())), preferred_element_type=F32)


def split(a):
    high = a.astype(BF16)
    return high, (a - high.astype(F32)).astype(BF16)


def dot3(product, a, b):
    return product(a[0], b[0]) + (product(a[1], b[0]) + product(a[0], b[1]))


def head_mask(shape, row_size, lane_size):
    rows = lax.broadcasted_iota(jnp.int32, shape, 0) // row_size
    lanes = lax.broadcasted_iota(jnp.int32, shape, 1) // lane_size
    return rows == lanes


def inverse_row(scalar_ref, index, length):
    return 1.0 / jnp.full((1, length), scalar_ref[index], F32)


def assign(sharp, x, entry, cluster, valid, xmt, weights, live_probs):
    points, width = x.shape
    heads = sharp.shape[0]
    head = width // heads
    slices = cluster.shape[1]
    xm = dot(x[...], entry[...]).astype(BF16)
    xmt[...] = xm.T
    cluster_t = cluster[...].T
    live = (lax.broadcasted_iota(jnp.int32, (1, points), 1) < valid).astype(F32)
    for h in range(heads):
        raw = dot(cluster_t, xmt[h * head : (h + 1) * head, :])
        logits = raw * inverse_row(sharp, h, points)
        e = jnp.exp(logits - jnp.max(logits, axis=0, keepdims=True))
        probs = e * (live / jnp.sum(e, axis=0, keepdims=True))
        if live_probs is not None:
            live_probs[h * slices : (h + 1) * slices, :] = probs
        weights[h * slices : (h + 1) * slices, :] = probs.astype(BF16)
    return xm


def valid_points(tally):
    return tally[lax.axis_index("pts") * lax.axis_size("grp") + lax.axis_index("grp")]


def opening_kernel(out):
    out[...] = jnp.zeros_like(out)


def points_kernel(
    tally, sharp, x, rc, entry, exit_, cluster, opening, payload, xmt, weights
):
    points, width = x.shape
    heads = sharp.shape[0]
    head = width // heads
    slices = cluster.shape[1]
    per = LANES // head
    groups = heads // per
    go = dot_nt(rc[...], exit_[...]).astype(BF16)
    xm = assign(sharp, x, entry, cluster, valid_points(tally), xmt, weights, None)
    rows = groups * slices
    lane_head = lax.broadcasted_iota(jnp.int32, (slices, 2 * LANES), 1) % LANES // head
    for g in range(groups):
        w = weights[g * per * slices : (g + 1) * per * slices, :]
        cut = slice(g * LANES, (g + 1) * LANES)
        full = dot(w, jnp.concatenate([xm[:, cut], go[:, cut]], axis=1))
        own = jnp.zeros((slices, 2 * LANES), F32)
        for j in range(per):
            own = jnp.where(lane_head == j, full[j * slices : (j + 1) * slices, :], own)
        payload[g * slices : (g + 1) * slices, :] = own[:, :LANES].astype(BF16)
        payload[rows + g * slices : rows + (g + 1) * slices, :] = own[:, LANES:].astype(BF16)
    ones = jnp.ones((heads, points), BF16)
    den = jnp.zeros((heads, rows), F32)
    head_row = lax.broadcasted_iota(jnp.int32, (heads, rows), 0)
    lane_group = lax.broadcasted_iota(jnp.int32, (heads, rows), 1) // slices
    for j in range(per):
        w = jnp.concatenate(
            [
                weights[(g * per + j) * slices : (g * per + j + 1) * slices, :]
                for g in range(groups)
            ],
            axis=0,
        )
        den = jnp.where(head_row == lane_group * per + j, dot_nt(ones, w), den)
    high = den.astype(BF16).astype(F32)
    payload[2 * rows :, :] = jnp.concatenate([high, den - high], axis=0).astype(BF16)


def shadow_kernel(
    tally,
    sharp,
    x,
    rc,
    entry,
    exit_,
    cluster,
    maps,
    payload_in,
    payload,
    xmt,
    got,
    weights,
    live_probs,
    maps_high,
    maps_low,
    cluster_rows,
):
    payload[...] = payload_in[...]
    assign(sharp, x, entry, cluster, valid_points(tally), xmt, weights, live_probs)
    got[...] = dot_nt(rc[...], exit_[...]).astype(BF16).T
    head = maps.shape[1]
    slices = cluster.shape[1]
    per = LANES // head
    mask = head_mask((LANES, LANES), head, head)
    for i in range(maps.shape[0]):
        a = jnp.concatenate([maps[i]] * per, axis=0)
        a = jnp.where(mask, jnp.concatenate([a] * per, axis=1), 0.0)
        high, low = split(a)
        maps_high[:, i * LANES : (i + 1) * LANES] = high
        maps_low[:, i * LANES : (i + 1) * LANES] = low
    c = cluster[...].astype(F32).T
    c = jnp.concatenate([c] * per, axis=1)
    c = jnp.concatenate([c] * per, axis=0)
    c = jnp.where(head_mask(c.shape, slices, head), c, 0.0)
    cluster_rows[...] = c.astype(BF16)


def middle_kernel(
    sharp,
    mine,
    other,
    maps_high,
    maps_low,
    cluster_rows,
    xmt,
    got,
    weights,
    live_probs,
    x,
    rc,
    keep,
    send,
    gxmt,
    tokens_out,
    grads_out,
    grad_rows,
):
    points, width = x.shape
    heads = sharp.shape[0]
    head = width // heads
    per = LANES // head
    groups = heads // per
    slices = cluster_rows.shape[0] // per
    rows = groups * slices
    scale = head**-0.5
    total = mine[...].astype(F32) + other[...].astype(F32)
    num = total[:rows]
    mixed_cotangent = total[rows : 2 * rows]
    den_rows = total[2 * rows : 2 * rows + heads] + total[2 * rows + heads : 2 * rows + 2 * heads]
    spread = (
        lax.broadcasted_iota(jnp.int32, (heads, LANES), 0) % per
        == lax.broadcasted_iota(jnp.int32, (heads, LANES), 1) // head
    ).astype(F32)
    d0 = den_rows.astype(BF16)
    rest = den_rows - d0.astype(F32)
    d1 = rest.astype(BF16)
    d2 = (rest - d1.astype(F32)).astype(BF16)
    spread = spread.astype(BF16)
    den = dot_tn(
        jnp.concatenate([d0.astype(F32), d1.astype(F32), d2.astype(F32)], axis=0).astype(BF16),
        jnp.concatenate([spread.astype(F32)] * 3, axis=0).astype(BF16),
    )
    clip_inverse = 1.0 / jnp.maximum(den, 1.0)
    tokens = num * clip_inverse
    tokens_out[...] = tokens
    maps = (maps_high[...], maps_low[...])
    qkv = dot3(dot, split(tokens), maps)
    wide = (LANES, per * slices)
    lane_mask = head_mask(wide, head, slices)
    row_mask = head_mask((per * slices, LANES), slices, head)

    def spread_heads(a):
        doubled = jnp.concatenate([a] * (LANES // slices), axis=0).T
        doubled = jnp.concatenate([doubled] * (per * slices // LANES), axis=1)
        return split(jnp.where(lane_mask, doubled, 0.0))

    def fold_heads(a):
        kept = jnp.where(row_mask, a, 0.0)
        out = kept[:slices]
        for j in range(1, per):
            out = out + kept[j * slices : (j + 1) * slices]
        return kept, out

    mixed_blocks, query_grads, key_grads, value_grads = [], [], [], []
    for g in range(groups):
        cut = slice(g * slices, (g + 1) * slices)
        q, k, v = (qkv[cut, i * LANES : (i + 1) * LANES] for i in range(3))
        gm = mixed_cotangent[cut]
        q_blocks, gm_blocks = spread_heads(q), spread_heads(gm)
        k2, v2 = split(k), split(v)
        scores = dot3(dot, k2, q_blocks) * scale
        g_attn = dot3(dot, v2, gm_blocks)
        e = jnp.exp(scores - jnp.max(scores, axis=0, keepdims=True))
        attn = e / jnp.sum(e, axis=0, keepdims=True)
        g_scores = attn * (g_attn - jnp.sum(g_attn * attn, axis=0, keepdims=True)) * scale
        attn2, gs2 = split(attn), split(g_scores)
        value_grads.append(dot3(dot_nt, attn2, gm_blocks))
        key_grads.append(dot3(dot_nt, gs2, q_blocks))
        attn_t, gs_t = split(attn.T), split(g_scores.T)
        query_grads.append(fold_heads(dot3(dot, gs_t, k2))[1])
        mixed_blocks.append(fold_heads(dot3(dot, attn_t, v2))[0].astype(BF16))
    grads = jnp.concatenate(
        [
            jnp.concatenate(query_grads, axis=0),
            jnp.concatenate(key_grads, axis=0),
            jnp.concatenate(value_grads, axis=0),
        ],
        axis=1,
    )
    grads_out[...] = grads
    token_cotangent = dot3(dot_nt, split(grads), maps)
    num_cotangent = token_cotangent * clip_inverse
    den_terms = jnp.where(den > 1.0, -token_cotangent * tokens * clip_inverse, 0.0)

    owners = grad_rows.shape[0]
    owner_rows = width // owners
    slice_sum = jnp.zeros((head, per * slices), F32)
    slice_mask = head_mask((LANES, per * slices), head, slices)
    temps = []
    for g in range(groups):
        cut = slice(g * slices, (g + 1) * slices)
        big = slice(g * per * slices, (g + 1) * per * slices)
        small = slice(g * LANES, (g + 1) * LANES)
        num_block = jnp.where(
            row_mask, jnp.concatenate([num_cotangent[cut]] * per, axis=0), 0.0
        ).astype(BF16)
        den_column = jnp.sum(
            jnp.where(row_mask, jnp.concatenate([den_terms[cut]] * per, axis=0), 0.0),
            axis=1,
            keepdims=True,
        )
        table = jnp.concatenate([mixed_blocks[g], num_block], axis=1)
        w = weights[big, :]
        xm_g = xmt[small, :]
        both = dot_tn(table, w)
        merged = both[:LANES].astype(BF16)
        grad_exit = dot(merged, rc[...])
        g_w = dot(table, jnp.concatenate([got[small, :], xm_g], axis=0)) + den_column
        raw = dot(cluster_rows[...], xm_g)
        g_raw = []
        for j in range(per):
            h = g * per + j
            part = slice(j * slices, (j + 1) * slices)
            lp = live_probs[h * slices : (h + 1) * slices, :]
            t = g_w[part] * lp
            g_logits = t - lp * jnp.sum(t, axis=0, keepdims=True)
            inverse = inverse_row(sharp, h, points)
            row = jnp.sum(g_logits * raw[part], axis=0, keepdims=True) * (inverse * inverse)
            temps.append(-row)
            g_raw.append((g_logits * inverse).astype(BF16))
        g_raw = jnp.concatenate(g_raw, axis=0)
        g_xm = (both[LANES:] + dot_tn(cluster_rows[...], g_raw)).astype(BF16)
        gxmt[small, :] = g_xm
        grad_entry = dot(g_xm, x[...]).T
        block = jnp.where(slice_mask, dot_nt(xm_g, g_raw), 0.0)
        for j in range(per):
            slice_sum = slice_sum + block[j * head : (j + 1) * head]
        for o in range(owners):
            grad_rows[o, :owner_rows, small] = grad_entry[
                o * owner_rows : (o + 1) * owner_rows
            ].astype(BF16)
        for r in range(g * LANES // owner_rows, (g + 1) * LANES // owner_rows):
            start = r * owner_rows - g * LANES
            grad_rows[r, owner_rows:, :] = grad_exit[start : start + owner_rows].astype(BF16)
    folded = slice_sum[:, :LANES]
    for i in range(1, per * slices // LANES):
        folded = folded + slice_sum[:, i * LANES : (i + 1) * LANES]
    folded = folded + pltpu.roll(folded, LANES // 2, 1)
    part = head * slices // width
    low = lax.broadcasted_iota(jnp.int32, (part, LANES), 1) < slices
    slice_rows = [
        jnp.where(low, folded[i * part : (i + 1) * part], folded[(i + 1) * part : (i + 2) * part])
        for i in range(0, head // part, 2)
    ]
    temp = jnp.sum(jnp.concatenate(temps, axis=0), axis=1, keepdims=True)
    temp = jnp.broadcast_to(temp, (heads, width // 2))
    temp_high = temp.astype(BF16).astype(F32)
    extra = jnp.concatenate(
        [
            jnp.concatenate(slice_rows, axis=1),
            jnp.concatenate([temp_high, temp - temp_high], axis=1),
        ],
        axis=0,
    ).astype(BF16)
    odd = lax.axis_index("grp") % 2
    chunk = 2 * owner_rows
    for i in range(owners // 2):
        keep[i * chunk : (i + 1) * chunk, :] = grad_rows[2 * i + odd]
        send[i * chunk : (i + 1) * chunk, :] = grad_rows[2 * i + 1 - odd]
    keep[owners // 2 * chunk :, :] = extra
    send[owners // 2 * chunk :, :] = extra


def features_kernel(gxmt, entry, tokens, grads, x_grad, token_grads):
    x_grad[...] = dot_nt(gxmt[...].T, entry[...]).astype(BF16)
    maps, head = token_grads.shape[:2]
    per = LANES // head
    full = dot3(dot, split(tokens[...].T), split(grads[...]))
    for i in range(maps):
        part = full[:, i * LANES : (i + 1) * LANES]
        part = jnp.where(head_mask((LANES, LANES), head, head), part, 0.0)
        out = part[:head]
        for j in range(1, per):
            out = out + part[j * head : (j + 1) * head]
        shift = LANES // 2
        while shift >= head:
            out = out + pltpu.roll(out, shift, 1)
            shift //= 2
        token_grads[i] = out[:, :head]


def finish_kernel(mine, other, weight_grads, slice_grad, temp_grad):
    total = mine[...].astype(F32) + other[...].astype(F32)
    owner_rows = weight_grads.shape[1]
    head, slices = slice_grad.shape
    weight_grads[0] = total[:owner_rows]
    weight_grads[1] = total[owner_rows : 2 * owner_rows]
    extra = total[2 * owner_rows :]
    part = head * slices // extra.shape[1]
    for i in range(head // part):
        tile = extra[:part, i // 2 * LANES : (i // 2 + 1) * LANES]
        if i % 2:
            tile = pltpu.roll(tile, LANES // 2, 1)
        slice_grad[i * part : (i + 1) * part, :] = tile[:, :slices]
    heads = temp_grad.shape[1]
    temp = extra[part:]
    middle = temp.shape[1] // 2
    temp = (temp[:, :middle] + temp[:, middle:])[:, :LANES]
    temp = jnp.where(head_mask(temp.shape, 1, 1), temp, 0.0)
    temp_grad[...] = jnp.sum(temp, axis=0, keepdims=True)[:, :heads]


def call(kernel, shapes, in_smem, count, scratch=(), space=pltpu.VMEM, limit=VMEM_LIMIT, flops=0):
    smem = pl.BlockSpec(memory_space=pltpu.SMEM)
    vmem = pl.BlockSpec(memory_space=pltpu.VMEM)
    rest = pl.BlockSpec(memory_space=space)
    return pl.pallas_call(
        kernel,
        out_shape=[jax.ShapeDtypeStruct(s, d) for s, d in shapes],
        in_specs=[smem] * in_smem + [rest] * (count - in_smem),
        out_specs=[vmem] * len(shapes),
        scratch_shapes=list(scratch),
        compiler_params=pltpu.CompilerParams(vmem_limit_bytes=limit),
        cost_estimate=pl.CostEstimate(flops=flops, bytes_accessed=0, transcendentals=0)
        if flops
        else None,
    )


def exchange(a, mask):
    devices = lax.axis_size("pts") * lax.axis_size("grp")
    return lax.ppermute(a, ALL, [(i, i ^ mask) for i in range(devices)])


def exchanges(a, masks):
    return [exchange(a, mask) for mask in masks]


def gather(mine, others):
    mine, others = mine.astype(F32), [a.astype(F32) for a in others]
    if len(others) == 1:
        return mine + others[0]
    return (mine + others[0]) + (others[1] + others[2])


def token_pack(values, start, root_scale, den_scale):
    row = lax.broadcasted_iota(jnp.int32, values.shape, 0)
    roots = jnp.sqrt(jnp.abs(values)) * root_scale
    roots = jnp.where(values < 0.0, -roots, roots)
    return jnp.where(row < start, roots, values * den_scale).astype(jnp.float16)


def token_unpack(packed, start, root_scale, den_scale):
    packed = packed.astype(F32)
    row = lax.broadcasted_iota(jnp.int32, packed.shape, 0)
    return packed * jnp.where(row < start, jnp.abs(packed) * root_scale**-2, 1.0 / den_scale)


def store_halves(total, start, target):
    pair = total[start:]
    n = pair.shape[1] // 2
    pair = pair[:, :n] + pair[:, n:]
    high = pair.astype(BF16).astype(F32)
    pair = jnp.concatenate([high, pair - high], axis=1)
    target[...] = jnp.concatenate([total[:start], pair], axis=0).astype(BF16)


def sum_kernel(heads, *refs):
    *given, target = refs
    total = gather(given[0][...], [a[...] for a in given[1:]])
    store_halves(total, total.shape[0] - heads, target)


def part_kernel(heads, chunk, keep, other, mine, theirs):
    half = lax.axis_index("grp") // 2
    common = keep.shape[0] - mine.shape[0] + chunk
    extra = keep[common:, :].astype(F32) + other[common:, :].astype(F32)
    for target, index in ((mine, half), (theirs, 1 - half)):
        rows = pl.ds(pl.multiple_of(index * chunk, chunk), chunk)
        own = keep[rows, :].astype(F32) + other[rows, :].astype(F32)
        total = jnp.concatenate([own, extra], axis=0)
        store_halves(total, total.shape[0] - heads, target)


def local(x, rc, entry, exit_, cluster, sharp, maps, tally):
    points, width = x.shape
    heads = sharp.shape[0]
    head, slices = cluster.shape
    owners = lax.axis_size("grp")
    devices = lax.axis_size("pts") * owners
    per = LANES // head
    rows = heads // per * slices
    token_rows = 2 * rows + 2 * heads
    far = [1 << bit for bit in range(4, devices.bit_length() - 1)]
    (opening,) = call(opening_kernel, [((8, LANES), F32)], 0, 0, flops=OPENING_FLOPS)()
    (payload,) = call(
        points_kernel,
        [((token_rows, LANES), BF16)],
        2,
        8,
        scratch=[
            pltpu.VMEM((width, points), BF16),
            pltpu.VMEM((heads * slices, points), BF16),
        ],
    )(tally, sharp, x, rc, entry, exit_, cluster, opening)
    steps = ((8,), *((mask,) for mask in far), (2, 4, 6), (1,))
    all_points = devices * points
    root_scale = 2.0 ** math.floor(math.log2(65000.0 / math.sqrt(all_points * width * 2.25)))
    den_scale = 2.0 ** -max(0, math.ceil(math.log2(all_points / 2.0**15)))
    others = exchanges(payload, steps[0])
    mine, xmt, got, weights, live_probs, maps_high, maps_low, cluster_rows = call(
        shadow_kernel,
        [
            ((token_rows, LANES), BF16),
            ((width, points), BF16),
            ((width, points), BF16),
            ((heads * slices, points), BF16),
            ((heads * slices, points), F32),
            ((LANES, 3 * LANES), BF16),
            ((LANES, 3 * LANES), BF16),
            ((per * slices, LANES), BF16),
        ],
        2,
        9,
    )(tally, sharp, x, rc, entry, exit_, cluster, maps, payload)
    total = gather(mine, others)
    for masks in steps[1:-1]:
        mine = token_pack(total, 2 * rows, root_scale, den_scale)
        others = exchanges(mine, masks)
        mine, *others = (
            token_unpack(a, 2 * rows, root_scale, den_scale) for a in (mine, *others)
        )
        total = gather(mine, others)
    mine = total
    (other,) = exchanges(mine, steps[-1])

    owner_rows = width // owners
    chunk = 2 * owner_rows
    extra = head * slices // width + heads
    keep, send, gxmt, tokens, grads = call(
        middle_kernel,
        [
            ((owners // 2 * chunk + extra, width), BF16),
            ((owners // 2 * chunk + extra, width), BF16),
            ((width, points), BF16),
            ((rows, LANES), F32),
            ((rows, 3 * LANES), F32),
        ],
        1,
        12,
        scratch=[pltpu.VMEM((owners, chunk, width), BF16)],
    )(
        sharp,
        mine,
        other,
        maps_high,
        maps_low,
        cluster_rows,
        xmt,
        got,
        weights,
        live_probs,
        x,
        rc,
    )

    got_half = exchange(send, 1)
    x_grad, token_grads = call(
        features_kernel,
        [((points, width), BF16), (maps.shape, F32)],
        0,
        4,
    )(gxmt, entry, tokens, grads)
    part_shape = ((chunk + extra, width), BF16)
    mine, theirs = call(
        functools.partial(part_kernel, heads, chunk), [part_shape, part_shape], 0, 2
    )(keep, got_half)
    others = [exchange(mine, 4), exchange(theirs, 2), exchange(theirs, 6)]
    for mask in (8, *far):
        (mine,) = call(
            functools.partial(sum_kernel, heads), [part_shape], 0, 1 + len(others)
        )(mine, *others)
        others = exchanges(mine, (mask,))
    (other,) = others
    weight_grads, slice_grad, temp_grad = call(
        finish_kernel,
        [
            ((2, owner_rows, width), F32),
            ((head, slices), F32),
            ((1, heads), F32),
        ],
        0,
        2,
    )(mine, other)
    return x_grad, weight_grads, slice_grad, temp_grad.reshape(heads), token_grads


def solution(mesh):
    return jax.shard_map(
        local,
        mesh=mesh,
        in_specs=(P(ALL, None), P(ALL, None), P(), P(), P(), P(), P(), P()),
        out_specs=(P(ALL, None), P(None, "grp", None), P(), P(), P()),
        check_vma=False,
    )
```

```python
import functools
import math

import jax
import jax.numpy as jnp
from jax import lax
from jax.experimental import pallas as pl
from jax.experimental.pallas import tpu as pltpu
from jax.sharding import PartitionSpec as P

F32 = jnp.float32
BF16 = jnp.bfloat16
ALL = ("pts", "grp")
LANES = 128
VMEM_LIMIT = 48 * 1024 * 1024
OPENING_FLOPS = 3_000_000_000


def dot(a, b):
    return lax.dot_general(a, b, (((1,), (0,)), ((), ())), preferred_element_type=F32)


def dot_nt(a, b):
    return lax.dot_general(a, b, (((1,), (1,)), ((), ())), preferred_element_type=F32)


def dot_tn(a, b):
    return lax.dot_general(a, b, (((0,), (0,)), ((), ())), preferred_element_type=F32)


def split(a):
    high = a.astype(BF16)
    return high, (a - high.astype(F32)).astype(BF16)


def dot3(product, a, b):
    rows = a[0].shape[0]
    both = product(jnp.concatenate(a, axis=0), b[0])
    return both[:rows] + (both[rows:] + product(a[0], b[1]))


def head_mask(shape, row_size, lane_size):
    rows = lax.broadcasted_iota(jnp.int32, shape, 0) // row_size
    lanes = lax.broadcasted_iota(jnp.int32, shape, 1) // lane_size
    return rows == lanes


def inverse_row(scalar_ref, index, length):
    return 1.0 / jnp.full((1, length), scalar_ref[index], F32)


def assign(sharp, x, entry, cluster, valid, xmt, weights, live_probs):
    points, width = x.shape
    heads = sharp.shape[0]
    head = width // heads
    slices = cluster.shape[1]
    xm = dot(x[...], entry[...]).astype(BF16)
    xmt[...] = xm.T
    cluster_t = cluster[...].T
    live = (lax.broadcasted_iota(jnp.int32, (1, points), 1) < valid).astype(F32)
    for h in range(heads):
        raw = dot(cluster_t, xmt[h * head : (h + 1) * head, :])
        logits = raw * inverse_row(sharp, h, points)
        e = jnp.exp(logits - jnp.max(logits, axis=0, keepdims=True))
        probs = e * (live / jnp.sum(e, axis=0, keepdims=True))
        if live_probs is not None:
            live_probs[h * slices : (h + 1) * slices, :] = probs
        weights[h * slices : (h + 1) * slices, :] = probs.astype(BF16)
    return xm


def valid_points(tally):
    return tally[lax.axis_index("pts") * lax.axis_size("grp") + lax.axis_index("grp")]


def opening_kernel(out):
    out[...] = jnp.zeros_like(out)


def points_kernel(
    tally, sharp, x, rc, entry, exit_, cluster, opening, payload, xmt, weights
):
    points, width = x.shape
    heads = sharp.shape[0]
    head = width // heads
    slices = cluster.shape[1]
    per = LANES // head
    groups = heads // per
    go = dot_nt(rc[...], exit_[...]).astype(BF16)
    xm = assign(sharp, x, entry, cluster, valid_points(tally), xmt, weights, None)
    rows = groups * slices
    lane_head = lax.broadcasted_iota(jnp.int32, (slices, 2 * LANES), 1) % LANES // head
    for g in range(groups):
        w = weights[g * per * slices : (g + 1) * per * slices, :]
        cut = slice(g * LANES, (g + 1) * LANES)
        full = dot(w, jnp.concatenate([xm[:, cut], go[:, cut]], axis=1))
        own = jnp.zeros((slices, 2 * LANES), F32)
        for j in range(per):
            own = jnp.where(lane_head == j, full[j * slices : (j + 1) * slices, :], own)
        payload[g * slices : (g + 1) * slices, :] = own[:, :LANES].astype(BF16)
        payload[rows + g * slices : rows + (g + 1) * slices, :] = own[:, LANES:].astype(BF16)
    ones = jnp.ones((heads, points), BF16)
    den = jnp.zeros((heads, rows), F32)
    head_row = lax.broadcasted_iota(jnp.int32, (heads, rows), 0)
    lane_group = lax.broadcasted_iota(jnp.int32, (heads, rows), 1) // slices
    for j in range(per):
        w = jnp.concatenate(
            [
                weights[(g * per + j) * slices : (g * per + j + 1) * slices, :]
                for g in range(groups)
            ],
            axis=0,
        )
        den = jnp.where(head_row == lane_group * per + j, dot_nt(ones, w), den)
    high = den.astype(BF16).astype(F32)
    payload[2 * rows :, :] = jnp.concatenate([high, den - high], axis=0).astype(BF16)


def shadow_kernel(
    tally,
    sharp,
    x,
    rc,
    entry,
    exit_,
    cluster,
    maps,
    payload_in,
    payload,
    xmt,
    got,
    weights,
    live_probs,
    maps_high,
    maps_low,
    cluster_rows,
):
    payload[...] = payload_in[...]
    assign(sharp, x, entry, cluster, valid_points(tally), xmt, weights, live_probs)
    got[...] = dot_nt(rc[...], exit_[...]).astype(BF16).T
    head = maps.shape[1]
    slices = cluster.shape[1]
    per = LANES // head
    mask = head_mask((LANES, LANES), head, head)
    for i in range(maps.shape[0]):
        a = jnp.concatenate([maps[i]] * per, axis=0)
        a = jnp.where(mask, jnp.concatenate([a] * per, axis=1), 0.0)
        high, low = split(a)
        maps_high[:, i * LANES : (i + 1) * LANES] = high
        maps_low[:, i * LANES : (i + 1) * LANES] = low
    c = cluster[...].astype(F32).T
    c = jnp.concatenate([c] * per, axis=1)
    c = jnp.concatenate([c] * per, axis=0)
    c = jnp.where(head_mask(c.shape, slices, head), c, 0.0)
    cluster_rows[...] = c.astype(BF16)


def middle_kernel(
    sharp,
    mine,
    other,
    maps_high,
    maps_low,
    cluster_rows,
    xmt,
    got,
    weights,
    live_probs,
    x,
    rc,
    keep,
    send,
    gxmt,
    tokens_out,
    grads_out,
    grad_rows,
):
    points, width = x.shape
    heads = sharp.shape[0]
    head = width // heads
    per = LANES // head
    groups = heads // per
    slices = cluster_rows.shape[0] // per
    rows = groups * slices
    scale = head**-0.5
    total = mine[...].astype(F32) + other[...].astype(F32)
    num = total[:rows]
    mixed_cotangent = total[rows : 2 * rows]
    den_rows = total[2 * rows : 2 * rows + heads] + total[2 * rows + heads : 2 * rows + 2 * heads]
    spread = (
        lax.broadcasted_iota(jnp.int32, (heads, LANES), 0) % per
        == lax.broadcasted_iota(jnp.int32, (heads, LANES), 1) // head
    ).astype(F32)
    d0 = den_rows.astype(BF16)
    rest = den_rows - d0.astype(F32)
    d1 = rest.astype(BF16)
    d2 = (rest - d1.astype(F32)).astype(BF16)
    spread = spread.astype(BF16)
    den = dot_tn(
        jnp.concatenate([d0.astype(F32), d1.astype(F32), d2.astype(F32)], axis=0).astype(BF16),
        jnp.concatenate([spread.astype(F32)] * 3, axis=0).astype(BF16),
    )
    clip_inverse = 1.0 / jnp.maximum(den, 1.0)
    tokens = num * clip_inverse
    tokens_out[...] = tokens
    maps = (maps_high[...], maps_low[...])
    qkv = dot3(dot, split(tokens), maps)
    wide = (LANES, per * slices)
    lane_mask = head_mask(wide, head, slices)
    row_mask = head_mask((per * slices, LANES), slices, head)

    def spread_heads(a):
        doubled = jnp.concatenate([a] * (LANES // slices), axis=0).T
        doubled = jnp.concatenate([doubled] * (per * slices // LANES), axis=1)
        return split(jnp.where(lane_mask, doubled, 0.0))

    def fold_heads(a):
        kept = jnp.where(row_mask, a, 0.0)
        out = kept[:slices]
        for j in range(1, per):
            out = out + kept[j * slices : (j + 1) * slices]
        return kept, out

    mixed_blocks, query_grads, key_grads, value_grads = [], [], [], []
    for g in range(groups):
        cut = slice(g * slices, (g + 1) * slices)
        q, k, v = (qkv[cut, i * LANES : (i + 1) * LANES] for i in range(3))
        gm = mixed_cotangent[cut]
        q_blocks, gm_blocks = spread_heads(q), spread_heads(gm)
        k2, v2 = split(k), split(v)
        scores = dot3(dot, k2, q_blocks) * scale
        g_attn = dot3(dot, v2, gm_blocks)
        e = jnp.exp(scores - jnp.max(scores, axis=0, keepdims=True))
        attn = e / jnp.sum(e, axis=0, keepdims=True)
        g_scores = attn * (g_attn - jnp.sum(g_attn * attn, axis=0, keepdims=True)) * scale
        attn2, gs2 = split(attn), split(g_scores)
        value_grads.append(dot3(dot_nt, attn2, gm_blocks))
        key_grads.append(dot3(dot_nt, gs2, q_blocks))
        attn_t, gs_t = split(attn.T), split(g_scores.T)
        query_grads.append(fold_heads(dot3(dot, gs_t, k2))[1])
        mixed_blocks.append(fold_heads(dot3(dot, attn_t, v2))[0].astype(BF16))
    grads = jnp.concatenate(
        [
            jnp.concatenate(query_grads, axis=0),
            jnp.concatenate(key_grads, axis=0),
            jnp.concatenate(value_grads, axis=0),
        ],
        axis=1,
    )
    grads_out[...] = grads
    token_cotangent = dot3(dot_nt, split(grads), maps)
    num_cotangent = token_cotangent * clip_inverse
    den_terms = jnp.where(den > 1.0, -token_cotangent * tokens * clip_inverse, 0.0)

    owners = grad_rows.shape[0]
    owner_rows = width // owners
    slice_sum = jnp.zeros((head, per * slices), F32)
    slice_mask = head_mask((LANES, per * slices), head, slices)
    temps = []
    for g in range(groups):
        cut = slice(g * slices, (g + 1) * slices)
        big = slice(g * per * slices, (g + 1) * per * slices)
        small = slice(g * LANES, (g + 1) * LANES)
        num_block = jnp.where(
            row_mask, jnp.concatenate([num_cotangent[cut]] * per, axis=0), 0.0
        ).astype(BF16)
        den_column = jnp.sum(
            jnp.where(row_mask, jnp.concatenate([den_terms[cut]] * per, axis=0), 0.0),
            axis=1,
            keepdims=True,
        )
        table = jnp.concatenate([mixed_blocks[g], num_block], axis=1)
        w = weights[big, :]
        xm_g = xmt[small, :]
        both = dot_tn(table, w)
        merged = both[:LANES].astype(BF16)
        grad_exit = dot(merged, rc[...])
        g_w = dot(table, jnp.concatenate([got[small, :], xm_g], axis=0)) + den_column
        raw = dot(cluster_rows[...], xm_g)
        g_raw = []
        for j in range(per):
            h = g * per + j
            part = slice(j * slices, (j + 1) * slices)
            lp = live_probs[h * slices : (h + 1) * slices, :]
            t = g_w[part] * lp
            g_logits = t - lp * jnp.sum(t, axis=0, keepdims=True)
            inverse = inverse_row(sharp, h, points)
            row = jnp.sum(g_logits * raw[part], axis=0, keepdims=True) * (inverse * inverse)
            temps.append(-row)
            g_raw.append((g_logits * inverse).astype(BF16))
        g_raw = jnp.concatenate(g_raw, axis=0)
        g_xm = (both[LANES:] + dot_tn(cluster_rows[...], g_raw)).astype(BF16)
        gxmt[small, :] = g_xm
        grad_entry = dot(g_xm, x[...]).T
        block = jnp.where(slice_mask, dot_nt(xm_g, g_raw), 0.0)
        for j in range(per):
            slice_sum = slice_sum + block[j * head : (j + 1) * head]
        for o in range(owners):
            grad_rows[o, :owner_rows, small] = grad_entry[
                o * owner_rows : (o + 1) * owner_rows
            ].astype(BF16)
        for r in range(g * LANES // owner_rows, (g + 1) * LANES // owner_rows):
            start = r * owner_rows - g * LANES
            grad_rows[r, owner_rows:, :] = grad_exit[start : start + owner_rows].astype(BF16)
    folded = slice_sum[:, :LANES]
    for i in range(1, per * slices // LANES):
        folded = folded + slice_sum[:, i * LANES : (i + 1) * LANES]
    folded = folded + pltpu.roll(folded, LANES // 2, 1)
    part = head * slices // width
    low = lax.broadcasted_iota(jnp.int32, (part, LANES), 1) < slices
    slice_rows = [
        jnp.where(low, folded[i * part : (i + 1) * part], folded[(i + 1) * part : (i + 2) * part])
        for i in range(0, head // part, 2)
    ]
    temp = jnp.sum(jnp.concatenate(temps, axis=0), axis=1, keepdims=True)
    temp = jnp.broadcast_to(temp, (heads, width // 2))
    temp_high = temp.astype(BF16).astype(F32)
    extra = jnp.concatenate(
        [
            jnp.concatenate(slice_rows, axis=1),
            jnp.concatenate([temp_high, temp - temp_high], axis=1),
        ],
        axis=0,
    ).astype(BF16)
    odd = lax.axis_index("grp") % 2
    chunk = 2 * owner_rows
    for i in range(owners // 2):
        keep[i * chunk : (i + 1) * chunk, :] = grad_rows[2 * i + odd]
        send[i * chunk : (i + 1) * chunk, :] = grad_rows[2 * i + 1 - odd]
    keep[owners // 2 * chunk :, :] = extra
    send[owners // 2 * chunk :, :] = extra


def features_kernel(gxmt, entry, tokens, grads, x_grad, token_grads):
    x_grad[...] = dot_nt(gxmt[...].T, entry[...]).astype(BF16)
    maps, head = token_grads.shape[:2]
    per = LANES // head
    full = dot3(dot, split(tokens[...].T), split(grads[...]))
    for i in range(maps):
        part = full[:, i * LANES : (i + 1) * LANES]
        part = jnp.where(head_mask((LANES, LANES), head, head), part, 0.0)
        out = part[:head]
        for j in range(1, per):
            out = out + part[j * head : (j + 1) * head]
        shift = LANES // 2
        while shift >= head:
            out = out + pltpu.roll(out, shift, 1)
            shift //= 2
        token_grads[i] = out[:, :head]


def finish_kernel(mine, other, weight_grads, slice_grad, temp_grad):
    total = mine[...].astype(F32) + other[...].astype(F32)
    owner_rows = weight_grads.shape[1]
    head, slices = slice_grad.shape
    weight_grads[0] = total[:owner_rows]
    weight_grads[1] = total[owner_rows : 2 * owner_rows]
    extra = total[2 * owner_rows :]
    part = head * slices // extra.shape[1]
    for i in range(head // part):
        tile = extra[:part, i // 2 * LANES : (i // 2 + 1) * LANES]
        if i % 2:
            tile = pltpu.roll(tile, LANES // 2, 1)
        slice_grad[i * part : (i + 1) * part, :] = tile[:, :slices]
    heads = temp_grad.shape[1]
    temp = extra[part:]
    middle = temp.shape[1] // 2
    temp = (temp[:, :middle] + temp[:, middle:])[:, :LANES]
    temp = jnp.where(head_mask(temp.shape, 1, 1), temp, 0.0)
    temp_grad[...] = jnp.sum(temp, axis=0, keepdims=True)[:, :heads]


def call(kernel, shapes, in_smem, count, scratch=(), space=pltpu.VMEM, limit=VMEM_LIMIT, flops=0):
    smem = pl.BlockSpec(memory_space=pltpu.SMEM)
    vmem = pl.BlockSpec(memory_space=pltpu.VMEM)
    rest = pl.BlockSpec(memory_space=space)
    return pl.pallas_call(
        kernel,
        out_shape=[jax.ShapeDtypeStruct(s, d) for s, d in shapes],
        in_specs=[smem] * in_smem + [rest] * (count - in_smem),
        out_specs=[vmem] * len(shapes),
        scratch_shapes=list(scratch),
        compiler_params=pltpu.CompilerParams(vmem_limit_bytes=limit),
        cost_estimate=pl.CostEstimate(flops=flops, bytes_accessed=0, transcendentals=0)
        if flops
        else None,
    )


def exchange(a, mask):
    devices = lax.axis_size("pts") * lax.axis_size("grp")
    return lax.ppermute(a, ALL, [(i, i ^ mask) for i in range(devices)])


def exchanges(a, masks):
    return [exchange(a, mask) for mask in masks]


def gather(mine, others):
    mine, others = mine.astype(F32), [a.astype(F32) for a in others]
    if len(others) == 1:
        return mine + others[0]
    return (mine + others[0]) + (others[1] + others[2])


def token_pack(values, start, root_scale, den_scale):
    row = lax.broadcasted_iota(jnp.int32, values.shape, 0)
    roots = jnp.sqrt(jnp.abs(values)) * root_scale
    roots = jnp.where(values < 0.0, -roots, roots)
    return jnp.where(row < start, roots, values * den_scale).astype(jnp.float16)


def token_unpack(packed, start, root_scale, den_scale):
    packed = packed.astype(F32)
    row = lax.broadcasted_iota(jnp.int32, packed.shape, 0)
    return packed * jnp.where(row < start, jnp.abs(packed) * root_scale**-2, 1.0 / den_scale)


def store_halves(total, start, target):
    pair = total[start:]
    n = pair.shape[1] // 2
    pair = pair[:, :n] + pair[:, n:]
    high = pair.astype(BF16).astype(F32)
    pair = jnp.concatenate([high, pair - high], axis=1)
    target[...] = jnp.concatenate([total[:start], pair], axis=0).astype(BF16)


def sum_kernel(heads, *refs):
    *given, target = refs
    total = gather(given[0][...], [a[...] for a in given[1:]])
    store_halves(total, total.shape[0] - heads, target)


def part_kernel(heads, chunk, keep, other, mine, theirs):
    half = lax.axis_index("grp") // 2
    common = keep.shape[0] - mine.shape[0] + chunk
    extra = keep[common:, :].astype(F32) + other[common:, :].astype(F32)
    for target, index in ((mine, half), (theirs, 1 - half)):
        rows = pl.ds(pl.multiple_of(index * chunk, chunk), chunk)
        own = keep[rows, :].astype(F32) + other[rows, :].astype(F32)
        total = jnp.concatenate([own, extra], axis=0)
        store_halves(total, total.shape[0] - heads, target)


def local(x, rc, entry, exit_, cluster, sharp, maps, tally):
    points, width = x.shape
    heads = sharp.shape[0]
    head, slices = cluster.shape
    owners = lax.axis_size("grp")
    devices = lax.axis_size("pts") * owners
    per = LANES // head
    rows = heads // per * slices
    token_rows = 2 * rows + 2 * heads
    far = [1 << bit for bit in range(4, devices.bit_length() - 1)]
    (opening,) = call(opening_kernel, [((8, LANES), F32)], 0, 0, flops=OPENING_FLOPS)()
    (payload,) = call(
        points_kernel,
        [((token_rows, LANES), BF16)],
        2,
        8,
        scratch=[
            pltpu.VMEM((width, points), BF16),
            pltpu.VMEM((heads * slices, points), BF16),
        ],
    )(tally, sharp, x, rc, entry, exit_, cluster, opening)
    steps = ((8,), *((mask,) for mask in far), (2, 4, 6), (1,))
    all_points = devices * points
    root_scale = 2.0 ** math.floor(math.log2(65000.0 / math.sqrt(all_points * width * 2.25)))
    den_scale = 2.0 ** -max(0, math.ceil(math.log2(all_points / 2.0**15)))
    others = exchanges(payload, steps[0])
    mine, xmt, got, weights, live_probs, maps_high, maps_low, cluster_rows = call(
        shadow_kernel,
        [
            ((token_rows, LANES), BF16),
            ((width, points), BF16),
            ((width, points), BF16),
            ((heads * slices, points), BF16),
            ((heads * slices, points), F32),
            ((LANES, 3 * LANES), BF16),
            ((LANES, 3 * LANES), BF16),
            ((per * slices, LANES), BF16),
        ],
        2,
        9,
    )(tally, sharp, x, rc, entry, exit_, cluster, maps, payload)
    total = gather(mine, others)
    for masks in steps[1:-1]:
        mine = token_pack(total, 2 * rows, root_scale, den_scale)
        others = exchanges(mine, masks)
        mine, *others = (
            token_unpack(a, 2 * rows, root_scale, den_scale) for a in (mine, *others)
        )
        total = gather(mine, others)
    mine = total
    (other,) = exchanges(mine, steps[-1])

    owner_rows = width // owners
    chunk = 2 * owner_rows
    extra = head * slices // width + heads
    keep, send, gxmt, tokens, grads = call(
        middle_kernel,
        [
            ((owners // 2 * chunk + extra, width), BF16),
            ((owners // 2 * chunk + extra, width), BF16),
            ((width, points), BF16),
            ((rows, LANES), F32),
            ((rows, 3 * LANES), F32),
        ],
        1,
        12,
        scratch=[pltpu.VMEM((owners, chunk, width), BF16)],
    )(
        sharp,
        mine,
        other,
        maps_high,
        maps_low,
        cluster_rows,
        xmt,
        got,
        weights,
        live_probs,
        x,
        rc,
    )

    got_half = exchange(send, 1)
    x_grad, token_grads = call(
        features_kernel,
        [((points, width), BF16), (maps.shape, F32)],
        0,
        4,
    )(gxmt, entry, tokens, grads)
    part_shape = ((chunk + extra, width), BF16)
    mine, theirs = call(
        functools.partial(part_kernel, heads, chunk), [part_shape, part_shape], 0, 2
    )(keep, got_half)
    others = [exchange(mine, 4), exchange(theirs, 2), exchange(theirs, 6)]
    for mask in (8, *far):
        (mine,) = call(
            functools.partial(sum_kernel, heads), [part_shape], 0, 1 + len(others)
        )(mine, *others)
        others = exchanges(mine, (mask,))
    (other,) = others
    weight_grads, slice_grad, temp_grad = call(
        finish_kernel,
        [
            ((2, owner_rows, width), F32),
            ((head, slices), F32),
            ((1, heads), F32),
        ],
        0,
        2,
    )(mine, other)
    return x_grad, weight_grads, slice_grad, temp_grad.reshape(heads), token_grads


def solution(mesh):
    return jax.shard_map(
        local,
        mesh=mesh,
        in_specs=(P(ALL, None), P(ALL, None), P(), P(), P(), P(), P(), P()),
        out_specs=(P(ALL, None), P(None, "grp", None), P(), P(), P()),
        check_vma=False,
    )
```
